256 devices in a mesh: dp: 8 (over z), shard: 32 (over y, x, core).
Axes of the slice: x: 4, y: 4, z: 8, core: 2. Of those that a mesh axis runs over, the one named last changes fastest.
Arguments:
- grads: bfloat16 [8, 64, 1024, 1024], P('dp', None, 'shard')
- left_factor: bfloat16 [256, 1024, 1024], P(('dp', 'shard'))
- right_factor: bfloat16 [256, 1024, 1024], P(('dp', 'shard'))
- momentum: bfloat16 [256, 1024, 1024], P(('dp', 'shard')), may hold values from -3 to 3
- block_order: int32 [64], replicated, may hold values from 0 to 63, each once
- owner_counts: int32 [32], replicated, may hold values from 1 to 8, 64 in all
Outputs:
- update: bfloat16 [64, 1024, 1024], P(None, 'shard', 'dp')
- new_momentum: bfloat16 [256, 1024, 1024], P(('dp', 'shard'))
The draws below stay inside these ranges and needn't reach their ends.
Inputs may be any that keep to these rules, and one draw needn't show every extreme that they name: Owner group o takes the owner_counts[o] entries of block_order after those of groups 0 to o - 1; its j-th block lives in slot j * 32 + o. `owner_counts`: the counts sum to 64; some group takes 8 blocks.
All inputs are finite; a program needn't handle non-finite values.
Results may differ from the reference program's by a relative error of at most 0.02.
Values may be sent and summed in bfloat16 or wider, within the bound.
A program may use at most 128 MiB of HBM per device.

```python
import math
import jax
import jax.numpy as jnp
import numpy as np
from jax import lax

BLOCK = 1024
BLOCKS = 64
SLOTS = 256
N_DP = 8
N_SHARD = 32


def block_scales(key):
    return 10.0 ** jax.random.uniform(key, (BLOCKS, BLOCK), jnp.float32)


def draw_grads(key, part):
    key = jax.random.fold_in(key, 11)
    key_noise, key_rows, key_cols = jax.random.split(key, 3)
    ramp = jnp.arange(BLOCK, dtype=jnp.float32) / BLOCK
    rise = 0.5 * math.log(3.0)
    row_scale = block_scales(key_rows)
    col_scale = block_scales(key_cols)
    noise = jnp.clip(jax.random.normal(key_noise, (N_DP, BLOCKS, BLOCK, BLOCK), jnp.float32), -4.0, 4.0)
    trend = jnp.exp(rise * ramp)
    rows_part = (row_scale * trend[None, :])[None, :, :, None]
    cols_part = (col_scale * trend[None, :])[None, :, None, :]
    return (noise * rows_part * cols_part).astype(jnp.bfloat16)


def factor_matrix(key, off_scale, lowest, highest):
    key_off, key_diag = jax.random.split(key)
    raw = jax.random.normal(key_off, (SLOTS, BLOCK, BLOCK), jnp.float32) * (off_scale / math.sqrt(BLOCK))
    mirrored = (raw + jnp.swapaxes(raw, 1, 2)) * math.sqrt(0.5)
    diagonal = jax.random.uniform(key_diag, (SLOTS, BLOCK), jnp.float32, lowest, highest)
    eye_mask = jnp.eye(BLOCK, dtype=jnp.float32)
    return (mirrored + eye_mask[None, :, :] * diagonal[:, :, None]).astype(jnp.bfloat16)


def draw_left_factor(key, part):
    key = jax.random.fold_in(key, 21)
    return factor_matrix(key, 0.8, 1.2, 3.0)


def draw_right_factor(key, part):
    key = jax.random.fold_in(key, 31)
    return factor_matrix(key, 0.8, 1.2, 3.0)


def level_of(own_key, shape, pieces, smallest, top_value):
    def one(dim, parts):
        heights = jax.random.uniform(jax.random.fold_in(jax.random.fold_in(own_key, 6), dim), (parts,), jnp.float32, smallest / len(pieces), top_value / len(pieces))
        return jnp.repeat(jnp.exp(heights), shape[dim] // parts).reshape((-1,) + (1,) * (len(shape) - dim - 1))

    loudness = one(*pieces[0])
    for cut in pieces[1:]:
        loudness = loudness * one(*cut)
    return loudness


def split_up(count, total, limit, skew):
    portions = [(1 << 20) // math.isqrt(grade ** skew) + 1 for grade in range(2, count + 1)]
    rest, holding = total - limit - (count - 1), [1] * (count - 1)
    while rest > 0:
        candidates = [i for i in range(count - 1) if holding[i] < limit]
        mass, budget = sum([portions[i] for i in candidates]), rest
        for i in candidates:
            addition = min(limit - holding[i], max(1, budget * portions[i] // mass), rest)
            holding[i] = holding[i] + addition
            rest = rest - addition
    return np.array([limit] + holding)


def uneven(stream_key, number_of, total, reach, slope):
    if number_of == 2:
        one = jax.random.randint(stream_key, (), max(1, total - reach), min(reach, total - 1) + 1)
        return jnp.stack([one, total - one])
    lengths = jnp.asarray(split_up(number_of, total, reach, slope), jnp.int32)
    twos = (number_of - 1) // 2
    donor, receiver = lengths[1:1 + 2 * twos:2], lengths[2:2 + 2 * twos:2]
    margin = jnp.minimum(donor - 1, reach - receiver)
    moved = jax.random.randint(jax.random.fold_in(stream_key, 1), (twos,), 0, 1 << 20) % (margin + 1)
    lengths = lengths.at[1:1 + 2 * twos:2].set(donor - moved).at[2:2 + 2 * twos:2].set(receiver + moved)
    return lengths[jax.random.permutation(jax.random.fold_in(stream_key, 2), number_of)]


def scatter_about(own_key, extent, width, bound, cuts=(), kind=jnp.bfloat16):
    level = level_of(own_key, extent, cuts, -0.22, 0.18) if cuts else 1.0
    array = jax.random.normal(own_key, extent, jnp.float32) * width * level
    return jnp.minimum(jnp.maximum(array, -bound), bound).astype(kind)


def setup_inputs(seed: int = 0) -> dict:
    splits = jax.random.split(jax.random.key(seed), 7)
    return {
        "grads": draw_grads(jax.random.fold_in(splits[6], 71), 0),
        "left_factor": draw_left_factor(jax.random.fold_in(splits[6], 71), 0),
        "right_factor": draw_right_factor(jax.random.fold_in(splits[6], 71), 0),
        "momentum": scatter_about(splits[3], (SLOTS, BLOCK, BLOCK), 0.5, 3.0, ((0, 256),)),
        "block_order": jax.random.permutation(splits[4], BLOCKS).astype(jnp.int32),
        "owner_counts": uneven(splits[5], N_SHARD, BLOCKS, N_DP, 2).astype(jnp.int32),
    }


def slot_of_blocks(block_order, owner_counts):
    finish = jnp.cumsum(owner_counts).astype(jnp.int32)
    starts = (finish - owner_counts).astype(jnp.int32)
    listing = jnp.arange(BLOCKS, dtype=jnp.int32)
    placed = jnp.zeros((BLOCKS,), jnp.int32).at[block_order].set(listing)
    owner = lax.optimization_barrier(jnp.sum((finish[None, :] <= placed[:, None]).astype(jnp.int32), axis=1)).astype(jnp.int32)
    within = (placed - starts[owner]).astype(jnp.int32)
    return (within * N_SHARD + owner).astype(jnp.int32)

def reference(grads, left_factor, right_factor, momentum, block_order, owner_counts):
    slot_ids = slot_of_blocks(block_order, owner_counts)

    def one_block(index):
        summed = lax.optimization_barrier(jnp.sum(grads[:, index].astype(jnp.float32), axis=0))
        grad_block = summed.astype(jnp.bfloat16)
        slot_id = slot_ids[index]
        inner_prod = jnp.dot(left_factor[slot_id], grad_block, preferred_element_type=jnp.float32).astype(jnp.bfloat16)
        outer_prod = jnp.dot(inner_prod, right_factor[slot_id], preferred_element_type=jnp.float32)
        grad_wide = grad_block.astype(jnp.float32)
        grad_square = jnp.sum(grad_wide * grad_wide)
        graft_scale = jnp.sqrt(grad_square / (BLOCK * BLOCK)) * lax.rsqrt(jnp.mean(outer_prod * outer_prod) + 1e-06)
        return (graft_scale * outer_prod, grad_square)
    directions, squares = lax.map(one_block, jnp.arange(BLOCKS, dtype=jnp.int32))
    clip_scale = jnp.minimum(1.0, 0.5 * lax.rsqrt(jnp.sum(squares) / (BLOCKS * BLOCK * BLOCK) + 1e-06))
    directions = clip_scale * directions
    momentum_next = 0.9 * momentum.astype(jnp.float32)
    momentum_next = momentum_next.at[slot_ids].add(directions)
    update = (-0.8 * (0.9 * momentum_next[slot_ids] + directions)).astype(jnp.bfloat16)
    return (update, momentum_next.astype(jnp.bfloat16))
```

```python
import functools

import jax
import jax.numpy as jnp
from jax import lax
from jax.experimental import pallas as pl
from jax.experimental.pallas import tpu as pltpu
from jax.sharding import PartitionSpec as P

MESH = pl.DeviceIdType.MESH
LAG = 4
SKEW = 3
F32 = jnp.float32
BF16 = jnp.bfloat16


class Plan:
    def __init__(self, planes, groups, blocks, rows, cols):
        self.planes, self.groups, self.blocks = planes, groups, blocks
        self.rows, self.cols = rows, cols
        extras = blocks - groups
        self.most = [groups] + [
            min(groups, (extras - (planes - 1 - j)) // j) for j in range(1, planes)
        ]
        self.base = [sum(self.most[:j]) for j in range(planes)]
        self.slots = sum(self.most)
        self.sends = max(extras - (planes - 2), LAG) + (planes - 2) * LAG
        self.listed = 2 * (self.sends + LAG)
        place = 0
        for name, size in (
            ("up", self.listed),
            ("down", self.listed),
            ("first", groups),
            ("rank", groups),
            ("slot", groups),
            ("where", blocks),
            ("spare", 1),
            ("scalars", 16),
        ):
            setattr(self, name, place)
            place += size
        self.size = place


def table_kernel(plan, order_ref, counts_ref, tab, held):
    n, g = plan.planes, plan.groups
    me, col = lax.axis_index("dp"), lax.axis_index("shard")
    prev, nxt = lax.rem(me + n - 1, n), lax.rem(me + 1, n)

    def clear(i, c):
        tab[i] = 0
        return c

    lax.fori_loop(0, plan.size, clear, 0)
    hist, desc, asc, rank, base, width = 0, 16, 32, 48, 64, 80
    for i in range(16):
        held[hist + i] = 0
        held[rank + i] = 0

    def tally(o, c):
        k = counts_ref[o]
        held[hist + k] = held[hist + k] + 1
        return c

    lax.fori_loop(0, g, tally, 0)
    run = jnp.int32(0)
    down_at = jnp.int32(0)
    widths = [None] * n
    for j in range(n - 1, -1, -1):
        run = run + held[hist + j + 1]
        widths[j] = jnp.int32(LAG) if j == 0 else jnp.maximum(run, LAG)
        held[desc + j] = down_at
        held[width + j] = widths[j]
        held[base + j] = plan.base[j]
        down_at = down_at + widths[j]
    total = down_at
    up_at = jnp.int32(0)
    for j in range(n):
        held[asc + j] = up_at
        up_at = up_at + widths[j]

    def group(o, p):
        count = counts_ref[o]

        def one(j, c):
            b = order_ref[p + j]
            r = held[rank + j]
            held[rank + j] = r + 1
            head = j == 0
            u = held[desc + j] + r
            tab[jnp.where(head, plan.spare, plan.up + u)] = b
            tab[jnp.where(head, plan.spare, plan.up + u + total)] = b
            v = held[asc + j] + r
            tab[jnp.where(head, plan.spare, plan.down + v)] = b
            tab[jnp.where(head, plan.spare, plan.down + v + total)] = b
            tab[jnp.where(head, plan.first + o, plan.spare)] = b
            tab[plan.where + b] = held[base + j] + r
            mine = j == me
            tab[jnp.where(mine, plan.rank + o, plan.spare)] = r
            tab[jnp.where(mine, plan.slot + r, plan.spare)] = o
            return c

        lax.fori_loop(0, count, one, 0)
        return p + count

    lax.fori_loop(0, g, group, jnp.int32(0))
    s = plan.scalars
    tab[s + 0] = held[desc + prev]
    tab[s + 1] = held[width + prev]
    tab[s + 2] = total - held[width + prev] - held[width + me]
    tab[s + 3] = held[asc + nxt]
    tab[s + 4] = held[width + nxt]
    tab[s + 5] = total - held[width + nxt] - held[width + me]
    tab[s + 6] = jnp.where(counts_ref[col] > me, 1, 0)


def step_kernel(
    plan,
    grads, left, right, momentum, tab,
    update, new_momentum,
    gp, gm, landp, landm, outp, outm, zp, zm, abuf, gblk,
    lv, rv, mv, inner, outer, nm, ubuf, cbuf, fbuf,
    sq_own, sq_mid, sqz, sqs,
    load_sem, ring_send, ring_recv, z_send, zp_recv, zm_recv, a_send, a_recv,
    q_send, q_recv, u_send, u_recv, f_send, f_recv,
    *rbufs,
):
    n, g, nb = plan.planes, plan.groups, plan.blocks
    rows, cols = plan.rows, plan.cols
    slab = rows // g
    half = slab // 2
    width = cols // n
    me, col = lax.axis_index("dp"), lax.axis_index("shard")
    ahead, behind = lax.rem(me + 1, n), lax.rem(me + n - 1, n)

    def loop(low, high, body):
        lax.fori_loop(low, high, lambda i, c: (body(i), c)[1], 0)

    def remote(src, dst, send, recv, dp, shard):
        return pltpu.make_async_remote_copy(
            src_ref=src, dst_ref=dst, send_sem=send, recv_sem=recv,
            device_id={"dp": dp, "shard": shard}, device_id_type=MESH,
        )

    load_p = pltpu.make_async_copy(grads.at[0, :, 0:half, :], gp.at[0:nb], load_sem.at[0])
    load_m = pltpu.make_async_copy(grads.at[0, :, half:slab, :], gm.at[0:nb], load_sem.at[1])
    load_p.start()
    load_m.start()
    loads = [
        pltpu.make_async_copy(src.at[0], dst, load_sem.at[2 + i])
        for i, (src, dst) in enumerate(((left, lv), (right, rv), (momentum, mv)))
    ]

    barrier = pltpu.get_barrier_semaphore()
    for a in range(1, n):
        pl.semaphore_signal(
            barrier, inc=1, device_id={"dp": lax.rem(me + a, n), "shard": col}, device_id_type=MESH
        )

    def greet(a):
        pl.semaphore_signal(
            barrier, inc=1, device_id={"dp": me, "shard": lax.rem(col + a, g)}, device_id_type=MESH
        )

    loop(1, g, greet)
    pl.semaphore_wait(barrier, n - 1 + g - 1)
    load_p.wait()
    load_m.wait()
    for load in loads:
        load.start()

    sc = plan.scalars
    ways = (
        (gp, landp, outp, 0, ahead, plan.up + tab[sc], tab[sc + 1]),
        (gm, landm, outm, 1, behind, plan.down + tab[sc + 3], tab[sc + 4]),
    )

    def passing(way, k):
        _, land, out, d, to, _, _ = way
        return remote(out.at[k], land.at[k], ring_send.at[d], ring_recv.at[d, k], to, col)

    def take(k):
        for way in ways:
            held, land, _, _, _, start, lag = way
            passing(way, k).wait_recv()
            own = held[tab[start + lag + k]]
            held[nb + k] = (land[k].astype(F32) + own.astype(F32)).astype(BF16)

    def give(k):
        for way in ways:
            held, _, out, _, _, start, lag = way
            source = jnp.where(k < lag, tab[start + k], nb + k - lag)
            out[k] = held[source]
            passing(way, k).start()

    loop(0, LAG, give)

    def both(k):
        take(k - LAG)
        give(k)

    loop(LAG, plan.sends, both)
    loop(plan.sends - LAG, plan.sends, take)

    def exchange(t):
        @pl.when(t == 0)
        def _():
            gblk[pl.ds(col * slab, slab), :] = abuf[0]

        @pl.when(t > 0)
        def _():
            remote(
                abuf.at[t], gblk.at[pl.ds(col * slab, slab), :], a_send, a_recv,
                me, lax.rem(t + col, g),
            ).start()

    far = SKEW * (n - 1)
    lines = (
        (gp, zp, 0, zp_recv, ahead, me - 1, 1),
        (gm, zm, 1, zm_recv, behind, n - 1 - me, n - 1),
    )

    def along(line, q):
        _, zbuf, d, recv, to, _, _ = line
        return remote(zbuf.at[q], zbuf.at[q], z_send.at[d], recv.at[q], to, col)

    def first_block(line, q):
        return line[0][tab[plan.first + lax.rem(q + col, g)]].astype(F32)

    def chain(t):
        @pl.when(me != 0)
        def _():
            for line in lines:
                zbuf, hops, source = line[1], line[5], line[6]
                q = t - SKEW * hops

                @pl.when((q >= 0) & (q < g))
                def _():
                    @pl.when(me == source)
                    def _():
                        zbuf[q] = first_block(line, q).astype(BF16)

                    @pl.when(me != source)
                    def _():
                        along(line, q).wait_recv()
                        zbuf[q] = (zbuf[q].astype(F32) + first_block(line, q)).astype(BF16)

                    along(line, q).start()

            @pl.when(t < g)
            def _():
                r = tab[plan.rank + lax.rem(t + col, g)]
                abuf[t, 0:half, :] = gp[nb + tab[sc + 2] + r]
                abuf[t, half:slab, :] = gm[nb + tab[sc + 5] + r]
                exchange(t)

        @pl.when((me == 0) & (t >= far))
        def _():
            q = t - far
            for line, low in zip(lines, (0, half)):
                along(line, q).wait_recv()
                abuf[q, low:low + half, :] = (
                    line[1][q].astype(F32) + first_block(line, q)
                ).astype(BF16)
            exchange(q)

    loop(0, g + far, chain)

    remote(
        gblk.at[0:(g - 1) * slab], gblk.at[0:(g - 1) * slab], a_send, a_recv, me, col
    ).wait_recv()
    filled = tab[sc + 6] > 0
    tile = min(128, rows)

    def square(i, acc):
        x = gblk[pl.ds(pl.multiple_of(i * tile, tile), tile), :].astype(F32)
        return acc + jnp.sum(x * x, axis=0, keepdims=True)

    grad_square = jnp.sum(lax.fori_loop(0, rows // tile, square, jnp.zeros((1, cols), F32)))
    own_tile = jnp.full((8, 128), grad_square, F32)
    sq_own[...] = jnp.where(filled, own_tile, 0.0)
    sqz[me] = sq_own[...]
    for a in range(1, n):
        to = lax.rem(me + a, n)
        remote(sq_own, sqz.at[me], q_send.at[0], q_recv.at[0], to, col).start()
    for load in loads:
        load.wait()
    strip = 256

    def first_product(i, c):
        at = pl.ds(pl.multiple_of(i * strip, strip), strip)
        inner[:, at] = jnp.dot(lv[...], gblk[:, at], preferred_element_type=F32).astype(BF16)
        return c

    lax.fori_loop(0, cols // strip, first_product, 0)
    remote(sqz.at[0:n - 1], sqz.at[0:n - 1], q_send.at[0], q_recv.at[0], me, col).wait_recv()
    mid = sqz[0]
    for j in range(1, n):
        mid = mid + sqz[j]
    sq_mid[...] = mid
    sqs[col] = mid

    def tell(a):
        remote(
            sq_mid, sqs.at[col], q_send.at[1], q_recv.at[1], me, lax.rem(col + a, g)
        ).start()

    loop(1, g, tell)

    def second_product(i, acc):
        at = pl.ds(pl.multiple_of(i * strip, strip), strip)
        x = jnp.dot(inner[...], rv[:, at], preferred_element_type=F32)
        outer[:, at] = x
        return acc + jnp.sum(x * x, axis=0, keepdims=True)

    outer_square = jnp.sum(
        lax.fori_loop(0, cols // strip, second_product, jnp.zeros((1, strip), F32))
    )
    remote(sqs.at[0:g - 1], sqs.at[0:g - 1], q_send.at[1], q_recv.at[1], me, col).wait_recv()
    total = lax.fori_loop(0, g, lambda j, acc: acc + sqs[j], jnp.zeros((8, 128), F32))
    cells = float(rows * cols)
    outer_tile = jnp.full((8, 128), outer_square, F32)
    graft = (jnp.sqrt(own_tile / cells) * lax.rsqrt(outer_tile / cells + 1e-06))[0:1, :]
    clip = jnp.minimum(1.0, 0.5 * lax.rsqrt(total / (nb * cells) + 1e-06))[0:1, :]

    pairs = [(n // 2, 0)] + [(n // 2 - i, n // 2 + i) for i in range(1, n // 2)]
    for q, pair in enumerate(pairs):
        def part(i):
            at = pl.ds(pl.multiple_of(i * tile, tile), tile)
            for h, a in enumerate(pair):
                lanes = pl.ds(pl.multiple_of(lax.rem(me + a, n) * width, width), width)
                direction = jnp.where(filled, clip * (graft * outer[at, lanes]), 0.0)
                following = 0.9 * mv[at, lanes].astype(F32) + direction
                nm[at, lanes] = following.astype(BF16)
                ubuf[q, at, h * width:(h + 1) * width] = (
                    -0.8 * (0.9 * following + direction)
                ).astype(BF16)

        loop(0, rows // tile, part)
        rbufs[q][col] = ubuf[q, pl.ds(col * slab, slab), :]

        def back(a):
            to = lax.rem(col + a, g)
            remote(
                ubuf.at[q, pl.ds(to * slab, slab), :], rbufs[q].at[col],
                u_send.at[q], u_recv.at[q], me, to,
            ).start()

        loop(1, g, back)

    store = pltpu.make_async_copy(nm, new_momentum.at[0], load_sem.at[5])
    store.start()

    def home(q, h, j, to):
        return remote(
            cbuf.at[2 * q + h, 0:plan.most[j]], fbuf.at[plan.base[j]:plan.base[j] + plan.most[j]],
            f_send.at[2 * q + h], f_recv.at[j], to, col,
        )

    for q, pair in enumerate(pairs):
        remote(
            rbufs[q].at[0:g - 1], rbufs[q].at[0:g - 1], u_send.at[q], u_recv.at[q], me, col
        ).wait_recv()

        def gather(r):
            piece = rbufs[q][tab[plan.slot + r]]
            cbuf[2 * q, r] = piece[:, 0:width]
            cbuf[2 * q + 1, r] = piece[:, width:2 * width]

        loop(0, g, gather)
        for j in range(n):
            @pl.when(me == j)
            def _():
                for h, a in enumerate(pair):
                    if a == 0:
                        fbuf[plan.base[j]:plan.base[j] + plan.most[j]] = (
                            cbuf[2 * q + h, 0:plan.most[j]]
                        )
                    else:
                        home(q, h, j, lax.rem(me + a, n)).start()

    for j in range(n):
        @pl.when(me != j)
        def _():
            home(0, 0, j, me).wait_recv()

    def place(b):
        update[b] = fbuf[tab[plan.where + b]]

    loop(0, nb, place)
    store.wait()
    for way in ways:
        remote(way[2], way[1], ring_send.at[way[3]], ring_recv.at[0, 0], me, col).wait_send()

    @pl.when(me != 0)
    def _():
        for line in lines:
            remote(line[1], line[1], z_send.at[line[2]], line[3].at[0], me, col).wait_send()

    remote(abuf.at[1:g], abuf.at[1:g], a_send, a_recv, me, col).wait_send()
    remote(sqz.at[0:n - 1], sqz.at[0:n - 1], q_send.at[0], q_recv.at[0], me, col).wait_send()
    remote(sqs.at[0:g - 1], sqs.at[0:g - 1], q_send.at[1], q_recv.at[1], me, col).wait_send()
    for q, pair in enumerate(pairs):
        remote(
            rbufs[q].at[0:g - 1], rbufs[q].at[0:g - 1], u_send.at[q], u_recv.at[q], me, col
        ).wait_send()
        for j in range(n):
            @pl.when(me == j)
            def _():
                for h, a in enumerate(pair):
                    if a != 0:
                        home(q, h, j, me).wait_send()


def per_device(planes, groups, grads, left, right, momentum, block_order, owner_counts):
    blocks, slab, cols = grads.shape[1:]
    rows = left.shape[1]
    plan = Plan(planes, groups, blocks, rows, cols)
    half, width = slab // 2, cols // planes
    smem = pl.BlockSpec(memory_space=pltpu.SMEM)
    table = pl.pallas_call(
        functools.partial(table_kernel, plan),
        out_shape=jax.ShapeDtypeStruct((plan.size,), jnp.int32),
        in_specs=[smem, smem],
        out_specs=smem,
        scratch_shapes=[pltpu.SMEM((96,), jnp.int32)],
    )(block_order, owner_counts)
    anywhere = pl.BlockSpec(memory_space=pl.ANY)
    dma = pltpu.SemaphoreType.DMA
    held = plan.blocks + plan.sends
    return pl.pallas_call(
        functools.partial(step_kernel, plan),
        out_shape=(
            jax.ShapeDtypeStruct((blocks, slab, width), BF16),
            jax.ShapeDtypeStruct((1, rows, cols), BF16),
        ),
        in_specs=[anywhere] * 4 + [smem],
        out_specs=(pl.BlockSpec(memory_space=pltpu.VMEM), anywhere),
        scratch_shapes=(
            [pltpu.VMEM((held, half, cols), BF16)] * 2
            + [pltpu.VMEM((plan.sends, half, cols), BF16)] * 4
            + [pltpu.VMEM((groups, half, cols), BF16)] * 2
            + [pltpu.VMEM((groups, slab, cols), BF16), pltpu.VMEM((rows, cols), BF16)]
            + [
                pltpu.VMEM((rows, rows), BF16),
                pltpu.VMEM((cols, cols), BF16),
                pltpu.VMEM((rows, cols), BF16),
                pltpu.VMEM((rows, cols), BF16),
                pltpu.VMEM((rows, cols), F32),
                pltpu.VMEM((rows, cols), BF16),
                pltpu.VMEM((planes // 2, rows, 2 * width), BF16),
                pltpu.VMEM((planes, groups, slab, width), BF16),
                pltpu.VMEM((plan.slots, slab, width), BF16),
                pltpu.VMEM((8, 128), F32),
                pltpu.VMEM((8, 128), F32),
                pltpu.VMEM((planes, 8, 128), F32),
                pltpu.VMEM((groups, 8, 128), F32),
            ]
            + [
                dma((6,)),
                dma((2,)),
                dma((2, plan.sends)),
                dma((2,)),
                dma((groups,)),
                dma((groups,)),
                dma,
                dma,
                dma((2,)),
                dma((2,)),
                dma((planes // 2,)),
                dma((planes // 2,)),
                dma((planes,)),
                dma((planes,)),
            ]
            + [pltpu.VMEM((groups, slab, 2 * width), BF16)] * (planes // 2)
        ),
        compiler_params=pltpu.CompilerParams(
            collective_id=0, has_side_effects=True, vmem_limit_bytes=56 * 1024 * 1024
        ),
        cost_estimate=pl.CostEstimate(
            flops=2 * rows * cols * (rows + cols), bytes_accessed=2 * 13 * rows * cols // 2,
            transcendentals=0,
        ),
    )(grads, left, right, momentum, table)


def solution(mesh):
    slots = P(("dp", "shard"), None, None)
    return jax.shard_map(
        functools.partial(per_device, mesh.shape["dp"], mesh.shape["shard"]),
        mesh=mesh,
        in_specs=(P("dp", None, "shard", None), slots, slots, slots, P(), P()),
        out_specs=(P(None, "shard", "dp"), slots),
        check_vma=False,
    )
```

```python
import functools

import jax
import jax.numpy as jnp
from jax import lax
from jax.experimental import pallas as pl
from jax.experimental.pallas import tpu as pltpu
from jax.sharding import PartitionSpec as P

MESH = pl.DeviceIdType.MESH
LAG = 2
SKEW = 3
EARLY = 9
F32 = jnp.float32
BF16 = jnp.bfloat16


class Plan:
    def __init__(self, planes, groups, blocks, rows, cols):
        self.planes, self.groups, self.blocks = planes, groups, blocks
        self.rows, self.cols = rows, cols
        extras = blocks - groups
        self.most = [groups] + [
            min(groups, (extras - (planes - 1 - j)) // j) for j in range(1, planes)
        ]
        self.base = [sum(self.most[:j]) for j in range(planes)]
        self.slots = sum(self.most)
        self.sends = max(extras - (planes - 2), LAG) + (planes - 2) * LAG
        place = 0
        for name, size in (
            ("before", self.sends),
            ("order", 2 * (self.sends + LAG)),
            ("first", groups),
            ("rank", groups),
            ("slot", groups),
            ("where", blocks),
            ("scalars", 16),
        ):
            setattr(self, name, place)
            place += size
        self.size = place


def table_kernel(plan, order_ref, counts_ref, tab, held):
    n, g = plan.planes, plan.groups
    me, col = lax.axis_index("dp"), lax.axis_index("shard")
    prev, nxt = lax.rem(me + n - 1, n), lax.rem(me + 1, n)
    hist, start, rank, width = 0, 16, 32, 48
    for i in range(plan.first):
        tab[i] = 0
    for i in range(16):
        held[hist + i] = 0
        held[rank + i] = 0

    def tally(o, seen):
        p, mine = seen
        k = counts_ref[o]
        held[hist + k] = held[hist + k] + 1
        b = order_ref[p]
        tab[plan.first + o] = b
        tab[plan.where + b] = o
        tab[plan.rank + o] = jnp.where(k > me, mine, 0)
        tab[plan.slot + o] = 0
        tab[plan.slot + mine] = o
        return p + k, mine + jnp.where(k > me, 1, 0)

    lax.fori_loop(0, g, tally, (jnp.int32(0), jnp.int32(0)))
    run = jnp.int32(0)
    at = jnp.int32(0)
    for j in range(n - 1, -1, -1):
        run = run + held[hist + j + 1]
        wide = jnp.int32(LAG) if j == 0 else jnp.maximum(run, LAG)
        held[start + j] = at
        held[width + j] = wide
        at = at + wide
    total = at
    for r in range(LAG):
        b = tab[plan.first + lax.rem(col + r, g)]
        tab[plan.order + held[start] + r] = b
        tab[plan.order + held[start] + r + total] = b

    def group(o, p):
        count = counts_ref[o]

        def one(j, c):
            b = order_ref[p + j]
            r = held[rank + j]
            held[rank + j] = r + 1
            u = plan.order + held[start + j] + r
            tab[u] = b
            tab[u + total] = b
            offset = jnp.int32(plan.base[1])
            for i in range(2, n):
                offset = jnp.where(j >= i, plan.base[i], offset)
            tab[plan.where + b] = offset + r
            return c

        lax.fori_loop(1, count, one, 0)
        return p + count

    lax.fori_loop(0, g, group, jnp.int32(0))
    s = plan.scalars
    before, after, own = held[width + prev], held[width + nxt], held[width + me]
    tab[s + 0] = plan.order + held[start + prev]
    tab[s + 1] = before
    tab[s + 2] = total - before - own
    tab[s + 3] = plan.order + held[start + nxt] + after - 1 + total
    tab[s + 4] = after
    tab[s + 5] = total - after - 1
    tab[s + 6] = jnp.where(counts_ref[col] > me, 1, 0)


def step_kernel(
    plan,
    grads, left, right, momentum, tab,
    pieces, new_momentum,
    gp, gm, landp, landm, outp, outm, zp, zm, abuf, gblk,
    lv, rv, mv, inner, outer, nm, ubuf, cbuf, fbuf,
    sq_own, sq_mid, sqz, sqs,
    load_sem, ring_send, ring_recv, z_send, zp_recv, zm_recv, a_send, a_recv,
    q_send, q_recv, u_send, u_recv, f_send, f_recv,
    *rbufs,
):
    n, g, nb = plan.planes, plan.groups, plan.blocks
    rows, cols = plan.rows, plan.cols
    slab = rows // g
    half = slab // 2
    width = cols // n
    me, col = lax.axis_index("dp"), lax.axis_index("shard")
    ahead, behind = lax.rem(me + 1, n), lax.rem(me + n - 1, n)

    def loop(low, high, body):
        lax.fori_loop(low, high, lambda i, c: (body(i), c)[1], 0)

    def remote(src, dst, send, recv, dp, shard):
        return pltpu.make_async_remote_copy(
            src_ref=src, dst_ref=dst, send_sem=send, recv_sem=recv,
            device_id={"dp": dp, "shard": shard}, device_id_type=MESH,
        )

    load_p = pltpu.make_async_copy(grads.at[0, :, 0:half, :], gp.at[0:nb], load_sem.at[0])
    load_m = pltpu.make_async_copy(grads.at[0, :, half:slab, :], gm.at[0:nb], load_sem.at[1])
    load_p.start()
    load_m.start()
    loads = [
        pltpu.make_async_copy(src.at[0], dst, load_sem.at[2 + i])
        for i, (src, dst) in enumerate(((left, lv), (right, rv), (momentum, mv)))
    ]

    barrier = pltpu.get_barrier_semaphore()
    for a in range(1, n):
        pl.semaphore_signal(
            barrier, inc=1, device_id={"dp": lax.rem(me + a, n), "shard": col}, device_id_type=MESH
        )

    def greet(a):
        pl.semaphore_signal(
            barrier, inc=1, device_id={"dp": me, "shard": lax.rem(col + a, g)}, device_id_type=MESH
        )

    loop(1, g, greet)
    pl.semaphore_wait(barrier, n - 1 + g - 1)
    load_p.wait()
    load_m.wait()
    for load in loads:
        load.start()

    sc = plan.scalars
    ways = (
        (gp, landp, outp, 0, ahead, tab[sc], 1, tab[sc + 1]),
        (gm, landm, outm, 1, behind, tab[sc + 3], -1, tab[sc + 4]),
    )
    parts = tuple(slice(h * (cols // 2), (h + 1) * (cols // 2)) for h in range(2))

    def passing(way, k, h):
        _, land, out, d, to, _, _, _ = way
        return remote(
            out.at[k, :, parts[h]], land.at[k, :, parts[h]],
            ring_send.at[d], ring_recv.at[2 * d + h, k], to, col,
        )

    def take(k, h):
        for way in ways:
            held, land, _, _, _, start, sign, lag = way
            passing(way, k, h).wait_recv()
            own = held[tab[jnp.maximum(start + sign * (lag + k), 0)], :, parts[h]]
            held[nb + k, :, parts[h]] = (
                land[k, :, parts[h]].astype(F32) + own.astype(F32)
            ).astype(BF16)

    def give(k, h):
        for way in ways:
            held, _, out, _, _, start, sign, lag = way
            source = jnp.where(k < lag, tab[jnp.maximum(start + sign * k, 0)], nb + k - lag)
            out[k, :, parts[h]] = held[source, :, parts[h]]
            passing(way, k, h).start()

    def ring(k, taking=True, giving=True):
        for h in range(2):
            if taking:
                take(k - LAG, h)
            if giving:
                give(k, h)

    def exchange(t):
        @pl.when(t == 0)
        def _():
            gblk[pl.ds(col * slab, slab), :] = abuf[0]

        @pl.when(t > 0)
        def _():
            remote(
                abuf.at[t], gblk.at[pl.ds(col * slab, slab), :], a_send, a_recv,
                me, lax.rem(t + col, g),
            ).start()

    far = SKEW * (n - 1)
    lines = (
        (gp, zp, 0, zp_recv, ahead, me - 1, 1),
        (gm, zm, 1, zm_recv, behind, n - 1 - me, n - 1),
    )
    begin, ready = max(plan.sends - EARLY, LAG), plan.sends + LAG
    end = max(begin + far + g - LAG, ready + g)

    def along(line, q):
        _, zbuf, d, recv, to, _, _ = line
        return remote(zbuf.at[q], zbuf.at[q], z_send.at[d], recv.at[q], to, col)

    def first_block(line, q):
        return line[0][tab[plan.first + lax.rem(q + col, g)]].astype(F32)

    def chain(t):
        @pl.when(me != 0)
        def _():
            for line in lines:
                zbuf, hops, source = line[1], line[5], line[6]
                q = t - begin - SKEW * hops + LAG

                @pl.when((q >= LAG) & (q < g))
                def _():
                    @pl.when(me == source)
                    def _():
                        zbuf[q] = first_block(line, q).astype(BF16)

                    @pl.when(me != source)
                    def _():
                        along(line, q).wait_recv()
                        zbuf[q] = (zbuf[q].astype(F32) + first_block(line, q)).astype(BF16)

                    along(line, q).start()

        @pl.when((me == 0) & (t >= begin + far) & (t < begin + far + g - LAG))
        def _():
            q = t - begin - far + LAG
            for line, low in zip(lines, (0, half)):
                along(line, q).wait_recv()
                abuf[q, low:low + half, :] = (
                    line[1][q].astype(F32) + first_block(line, q)
                ).astype(BF16)
            exchange(q)

    def settle(t):
        i = t - ready

        @pl.when((i < g) & ((me != 0) | (i < LAG)))
        def _():
            r = jnp.where(me == 0, i, tab[plan.rank + lax.rem(i + col, g)])
            abuf[i, 0:half, :] = gp[nb + tab[sc + 2] + r]
            abuf[i, half:slab, :] = gm[nb + tab[sc + 5] - r]
            exchange(i)

    loop(0, LAG, lambda k: ring(k, taking=False))
    loop(LAG, begin, ring)
    loop(begin, plan.sends, lambda k: (ring(k), chain(k)))
    loop(plan.sends, ready, lambda k: (ring(k, giving=False), chain(k)))
    loop(ready, end, lambda k: (chain(k), settle(k)))

    remote(
        gblk.at[0:(g - 1) * slab], gblk.at[0:(g - 1) * slab], a_send, a_recv, me, col
    ).wait_recv()
    filled = tab[sc + 6] > 0
    tile = min(128, rows)

    def square(i, acc):
        x = gblk[pl.ds(pl.multiple_of(i * tile, tile), tile), :].astype(F32)
        return acc + jnp.sum(x * x, axis=0, keepdims=True)

    grad_square = jnp.sum(lax.fori_loop(0, rows // tile, square, jnp.zeros((1, cols), F32)))
    own_tile = jnp.full((8, 128), grad_square, F32)
    sq_own[...] = jnp.where(filled, own_tile, 0.0)
    sqz[me] = sq_own[...]
    for a in range(1, n):
        to = lax.rem(me + a, n)
        remote(sq_own, sqz.at[me], q_send.at[0], q_recv.at[0], to, col).start()
    for load in loads:
        load.wait()
    strip = 256

    def first_product(i, c):
        at = pl.ds(pl.multiple_of(i * strip, strip), strip)
        inner[:, at] = jnp.dot(lv[...], gblk[:, at], preferred_element_type=F32).astype(BF16)
        return c

    lax.fori_loop(0, cols // strip, first_product, 0)
    remote(sqz.at[0:n - 1], sqz.at[0:n - 1], q_send.at[0], q_recv.at[0], me, col).wait_recv()
    mid = sqz[0]
    for j in range(1, n):
        mid = mid + sqz[j]
    sq_mid[...] = mid
    sqs[col] = mid

    def tell(a):
        remote(
            sq_mid, sqs.at[col], q_send.at[1], q_recv.at[1], me, lax.rem(col + a, g)
        ).start()

    loop(1, g, tell)

    def second_product(i, acc):
        at = pl.ds(pl.multiple_of(i * strip, strip), strip)
        x = jnp.dot(inner[...], rv[:, at], preferred_element_type=F32)
        outer[:, at] = x
        return acc + jnp.sum(x * x, axis=0, keepdims=True)

    outer_square = jnp.sum(
        lax.fori_loop(0, cols // strip, second_product, jnp.zeros((1, strip), F32))
    )
    remote(sqs.at[0:g - 1], sqs.at[0:g - 1], q_send.at[1], q_recv.at[1], me, col).wait_recv()
    total = lax.fori_loop(0, g, lambda j, acc: acc + sqs[j], jnp.zeros((8, 128), F32))
    cells = float(rows * cols)
    outer_tile = jnp.full((8, 128), outer_square, F32)
    graft = (jnp.sqrt(own_tile / cells) * lax.rsqrt(outer_tile / cells + 1e-06))[0:1, :]
    clip = jnp.minimum(1.0, 0.5 * lax.rsqrt(total / (nb * cells) + 1e-06))[0:1, :]

    pairs = [(n // 2, 0)] + [(n // 2 - i, n // 2 + i) for i in range(1, n // 2)]
    def home(q, h, j, to):
        return remote(
            cbuf.at[2 * q + h, 0:plan.most[j]], fbuf.at[plan.base[j]:plan.base[j] + plan.most[j]],
            f_send.at[2 * q + h], f_recv.at[j], to, col,
        )

    def outward(q, pair):
        def part(i):
            at = pl.ds(pl.multiple_of(i * tile, tile), tile)
            for h, a in enumerate(pair):
                lanes = pl.ds(pl.multiple_of(lax.rem(me + a, n) * width, width), width)
                direction = jnp.where(filled, clip * (graft * outer[at, lanes]), 0.0)
                following = 0.9 * mv[at, lanes].astype(F32) + direction
                nm[at, lanes] = following.astype(BF16)
                ubuf[q, at, h * width:(h + 1) * width] = (
                    -0.8 * (0.9 * following + direction)
                ).astype(BF16)

        loop(0, rows // tile, part)
        rbufs[q][col] = ubuf[q, pl.ds(col * slab, slab), :]

        def back(a):
            to = lax.rem(col + a, g)
            remote(
                ubuf.at[q, pl.ds(to * slab, slab), :], rbufs[q].at[col],
                u_send.at[q], u_recv.at[q], me, to,
            ).start()

        loop(1, g, back)

    def homeward(q, pair):
        remote(
            rbufs[q].at[0:g - 1], rbufs[q].at[0:g - 1], u_send.at[q], u_recv.at[q], me, col
        ).wait_recv()

        def gather(r):
            piece = rbufs[q][tab[plan.slot + r]]
            cbuf[2 * q, r] = piece[:, 0:width]
            cbuf[2 * q + 1, r] = piece[:, width:2 * width]

        loop(0, g, gather)
        for j in range(n):
            @pl.when(me == j)
            def _():
                for h, a in enumerate(pair):
                    if a == 0:
                        fbuf[plan.base[j]:plan.base[j] + plan.most[j]] = (
                            cbuf[2 * q + h, 0:plan.most[j]]
                        )
                    else:
                        home(q, h, j, lax.rem(me + a, n)).start()

    for q, pair in enumerate(pairs):
        outward(q, pair)
        if q > 0:
            homeward(q - 1, pairs[q - 1])
    store = pltpu.make_async_copy(nm, new_momentum.at[0], load_sem.at[5])
    store.start()
    homeward(len(pairs) - 1, pairs[-1])

    for j in range(n):
        @pl.when(me != j)
        def _():
            home(0, 0, j, me).wait_recv()

    keep = pltpu.make_async_copy(fbuf, pieces, load_sem.at[0])
    keep.start()
    store.wait()
    keep.wait()
    for way in ways:
        remote(way[2], way[1], ring_send.at[way[3]], ring_recv.at[0, 0], me, col).wait_send()

    @pl.when(me != 0)
    def _():
        for line in lines:
            remote(
                line[1].at[LAG:g], line[1].at[LAG:g], z_send.at[line[2]], line[3].at[0], me, col
            ).wait_send()

    remote(abuf.at[1:g], abuf.at[1:g], a_send, a_recv, me, col).wait_send()
    remote(sqz.at[0:n - 1], sqz.at[0:n - 1], q_send.at[0], q_recv.at[0], me, col).wait_send()
    remote(sqs.at[0:g - 1], sqs.at[0:g - 1], q_send.at[1], q_recv.at[1], me, col).wait_send()
    for q, pair in enumerate(pairs):
        remote(
            rbufs[q].at[0:g - 1], rbufs[q].at[0:g - 1], u_send.at[q], u_recv.at[q], me, col
        ).wait_send()
        for j in range(n):
            @pl.when(me == j)
            def _():
                for h, a in enumerate(pair):
                    if a != 0:
                        home(q, h, j, me).wait_send()


def last_kernel(plan, pieces, following, tab, update, new_momentum, sems):
    step = plan.rows // 4
    copies = [
        pltpu.make_async_copy(
            following.at[0, i * step:(i + 1) * step], new_momentum.at[0, i * step:(i + 1) * step],
            sems.at[i],
        )
        for i in range(4)
    ]
    for copy in copies:
        copy.start()

    def place(b, c):
        update[b] = pieces[tab[plan.where + b]]
        return c

    lax.fori_loop(0, plan.blocks, place, 0)
    for copy in copies:
        copy.wait()


def per_device(planes, groups, grads, left, right, momentum, block_order, owner_counts):
    blocks, slab, cols = grads.shape[1:]
    rows = left.shape[1]
    plan = Plan(planes, groups, blocks, rows, cols)
    half, width = slab // 2, cols // planes
    smem = pl.BlockSpec(memory_space=pltpu.SMEM)
    table = pl.pallas_call(
        functools.partial(table_kernel, plan),
        out_shape=jax.ShapeDtypeStruct((plan.size,), jnp.int32),
        in_specs=[smem, smem],
        out_specs=smem,
        scratch_shapes=[pltpu.SMEM((64,), jnp.int32)],
    )(block_order, owner_counts)
    anywhere = pl.BlockSpec(memory_space=pl.ANY)
    dma = pltpu.SemaphoreType.DMA
    held = plan.blocks + plan.sends
    pieces, following = pl.pallas_call(
        functools.partial(step_kernel, plan),
        out_shape=(
            jax.ShapeDtypeStruct((plan.slots, slab, width), BF16),
            jax.ShapeDtypeStruct((1, rows, cols), BF16),
        ),
        in_specs=[anywhere] * 4 + [smem],
        out_specs=(anywhere, anywhere),
        scratch_shapes=(
            [pltpu.VMEM((held, half, cols), BF16)] * 2
            + [pltpu.VMEM((plan.sends, half, cols), BF16)] * 4
            + [pltpu.VMEM((groups, half, cols), BF16)] * 2
            + [pltpu.VMEM((groups, slab, cols), BF16), pltpu.VMEM((rows, cols), BF16)]
            + [
                pltpu.VMEM((rows, rows), BF16),
                pltpu.VMEM((cols, cols), BF16),
                pltpu.VMEM((rows, cols), BF16),
                pltpu.VMEM((rows, cols), BF16),
                pltpu.VMEM((rows, cols), F32),
                pltpu.VMEM((rows, cols), BF16),
                pltpu.VMEM((planes // 2, rows, 2 * width), BF16),
                pltpu.VMEM((planes, groups, slab, width), BF16),
                pltpu.VMEM((plan.slots, slab, width), BF16),
                pltpu.VMEM((8, 128), F32),
                pltpu.VMEM((8, 128), F32),
                pltpu.VMEM((planes, 8, 128), F32),
                pltpu.VMEM((groups, 8, 128), F32),
            ]
            + [
                dma((6,)),
                dma((2,)),
                dma((4, plan.sends)),
                dma((2,)),
                dma((groups,)),
                dma((groups,)),
                dma,
                dma,
                dma((2,)),
                dma((2,)),
                dma((planes // 2,)),
                dma((planes // 2,)),
                dma((planes,)),
                dma((planes,)),
            ]
            + [pltpu.VMEM((groups, slab, 2 * width), BF16)] * (planes // 2)
        ),
        compiler_params=pltpu.CompilerParams(
            collective_id=0, has_side_effects=True, vmem_limit_bytes=56 * 1024 * 1024
        ),
        cost_estimate=pl.CostEstimate(
            flops=2 * rows * cols * (rows + cols), bytes_accessed=2 * 13 * rows * cols // 2,
            transcendentals=0,
        ),
    )(grads, left, right, momentum, table)
    return pl.pallas_call(
        functools.partial(last_kernel, plan),
        out_shape=(
            jax.ShapeDtypeStruct((blocks, slab, width), BF16),
            jax.ShapeDtypeStruct((1, rows, cols), BF16),
        ),
        in_specs=[pl.BlockSpec(memory_space=pltpu.VMEM), anywhere, smem],
        out_specs=(pl.BlockSpec(memory_space=pltpu.VMEM), anywhere),
        scratch_shapes=[dma((4,))],
    )(pieces, following, table)


def solution(mesh):
    slots = P(("dp", "shard"), None, None)
    return jax.shard_map(
        functools.partial(per_device, mesh.shape["dp"], mesh.shape["shard"]),
        mesh=mesh,
        in_specs=(P("dp", None, "shard", None), slots, slots, slots, P(), P()),
        out_specs=(P(None, "shard", "dp"), slots),
        check_vma=False,
    )
```

```python
import functools

import jax
import jax.numpy as jnp
from jax import lax
from jax.experimental import pallas as pl
from jax.experimental.pallas import tpu as pltpu
from jax.sharding import PartitionSpec as P

MESH = pl.DeviceIdType.MESH
LAG = 4
PARTS = 1
SKEW = 4
EARLY = 24
F32 = jnp.float32
BF16 = jnp.bfloat16


class Plan:
    def __init__(self, planes, groups, blocks, rows, cols):
        self.planes, self.groups, self.blocks = planes, groups, blocks
        self.rows, self.cols = rows, cols
        extras = blocks - groups
        self.most = [groups] + [
            min(groups, (extras - (planes - 1 - j)) // j) for j in range(1, planes)
        ]
        self.base = [sum(self.most[:j]) for j in range(planes)]
        self.slots = sum(self.most)
        self.sends = max(extras - (planes - 2), LAG) + (planes - 2) * LAG
        place = 0
        for name, size in (
            ("before", self.sends),
            ("order", 2 * (self.sends + LAG)),
            ("first", groups),
            ("rank", groups),
            ("slot", groups),
            ("where", blocks),
            ("scalars", 16),
        ):
            setattr(self, name, place)
            place += size
        self.size = place


def table_kernel(plan, order_ref, counts_ref, tab, held):
    n, g = plan.planes, plan.groups
    me, col = lax.axis_index("dp"), lax.axis_index("shard")
    prev, nxt = lax.rem(me + n - 1, n), lax.rem(me + 1, n)
    hist, start, rank, width = 0, 16, 32, 48
    for i in range(plan.first):
        tab[i] = 0
    for i in range(16):
        held[hist + i] = 0
        held[rank + i] = 0

    def tally(o, seen):
        p, mine = seen
        k = counts_ref[o]
        held[hist + k] = held[hist + k] + 1
        b = order_ref[p]
        tab[plan.first + o] = b
        tab[plan.where + b] = o
        tab[plan.rank + o] = jnp.where(k > me, mine, 0)
        tab[plan.slot + o] = 0
        tab[plan.slot + mine] = o
        return p + k, mine + jnp.where(k > me, 1, 0)

    lax.fori_loop(0, g, tally, (jnp.int32(0), jnp.int32(0)))
    run = jnp.int32(0)
    at = jnp.int32(0)
    for j in range(n - 1, -1, -1):
        run = run + held[hist + j + 1]
        wide = jnp.int32(LAG) if j == 0 else jnp.maximum(run, LAG)
        held[start + j] = at
        held[width + j] = wide
        at = at + wide
    total = at
    for r in range(LAG):
        b = tab[plan.first + lax.rem(col + r, g)]
        tab[plan.order + held[start] + r] = b
        tab[plan.order + held[start] + r + total] = b

    def group(o, p):
        count = counts_ref[o]

        def one(j, c):
            b = order_ref[p + j]
            r = held[rank + j]
            held[rank + j] = r + 1
            u = plan.order + held[start + j] + r
            tab[u] = b
            tab[u + total] = b
            offset = jnp.int32(plan.base[1])
            for i in range(2, n):
                offset = jnp.where(j >= i, plan.base[i], offset)
            tab[plan.where + b] = offset + r
            return c

        lax.fori_loop(1, count, one, 0)
        return p + count

    lax.fori_loop(0, g, group, jnp.int32(0))
    s = plan.scalars
    before, after, own = held[width + prev], held[width + nxt], held[width + me]
    tab[s + 0] = plan.order + held[start + prev]
    tab[s + 1] = before
    tab[s + 2] = total - before - own
    tab[s + 3] = plan.order + held[start + nxt] + after - 1 + total
    tab[s + 4] = after
    tab[s + 5] = total - after - 1
    tab[s + 6] = jnp.where(counts_ref[col] > me, 1, 0)


def step_kernel(
    plan,
    grads, left, right, momentum, tab,
    pieces, new_momentum,
    gp, gm, landp, landm, outp, outm, zp, zm, abuf, gblk,
    lv, rv, mv, inner, outer, nm, ubuf, cbuf, fbuf,
    sq_own, sq_mid, sqz, sqs,
    load_sem, ring_send, ring_recv, z_send, zp_recv, zm_recv, a_send, a_recv,
    q_send, q_recv, u_send, u_recv, f_send, f_recv,
    *rbufs,
):
    n, g, nb = plan.planes, plan.groups, plan.blocks
    rows, cols = plan.rows, plan.cols
    slab = rows // g
    half = slab // 2
    width = cols // n
    me, col = lax.axis_index("dp"), lax.axis_index("shard")
    ahead, behind = lax.rem(me + 1, n), lax.rem(me + n - 1, n)

    def loop(low, high, body):
        lax.fori_loop(low, high, lambda i, c: (body(i), c)[1], 0)

    def remote(src, dst, send, recv, dp, shard):
        return pltpu.make_async_remote_copy(
            src_ref=src, dst_ref=dst, send_sem=send, recv_sem=recv,
            device_id={"dp": dp, "shard": shard}, device_id_type=MESH,
        )

    load_p = pltpu.make_async_copy(grads.at[0, :, 0:half, :], gp.at[0:nb], load_sem.at[0])
    load_m = pltpu.make_async_copy(grads.at[0, :, half:slab, :], gm.at[0:nb], load_sem.at[1])
    load_p.start()
    load_m.start()
    loads = [
        pltpu.make_async_copy(src.at[0], dst, load_sem.at[2 + i])
        for i, (src, dst) in enumerate(((left, lv), (right, rv), (momentum, mv)))
    ]

    barrier = pltpu.get_barrier_semaphore()
    for a in range(1, n):
        pl.semaphore_signal(
            barrier, inc=1, device_id={"dp": lax.rem(me + a, n), "shard": col}, device_id_type=MESH
        )

    def greet(a):
        pl.semaphore_signal(
            barrier, inc=1, device_id={"dp": me, "shard": lax.rem(col + a, g)}, device_id_type=MESH
        )

    loop(1, g, greet)
    pl.semaphore_wait(barrier, n - 1 + g - 1)
    load_p.wait()
    load_m.wait()
    for load in loads:
        load.start()

    sc = plan.scalars
    ways = (
        (gp, landp, outp, 0, ahead, tab[sc], 1, tab[sc + 1]),
        (gm, landm, outm, 1, behind, tab[sc + 3], -1, tab[sc + 4]),
    )
    parts = tuple(slice(h * (cols // PARTS), (h + 1) * (cols // PARTS)) for h in range(PARTS))

    def passing(way, k, h):
        _, land, out, d, to, _, _, _ = way
        return remote(
            out.at[k, :, parts[h]], land.at[k, :, parts[h]],
            ring_send.at[d], ring_recv.at[PARTS * d + h, k], to, col,
        )

    def take(k, h):
        for way in ways:
            held, land, _, _, _, start, sign, lag = way
            passing(way, k, h).wait_recv()
            own = held[tab[jnp.maximum(start + sign * (lag + k), 0)], :, parts[h]]
            held[nb + k, :, parts[h]] = (
                land[k, :, parts[h]].astype(F32) + own.astype(F32)
            ).astype(BF16)

    def give(k, h):
        for way in ways:
            held, _, out, _, _, start, sign, lag = way
            source = jnp.where(k < lag, tab[jnp.maximum(start + sign * k, 0)], nb + k - lag)
            out[k, :, parts[h]] = held[source, :, parts[h]]
            passing(way, k, h).start()

    def ring(k, taking=True, giving=True):
        for h in range(PARTS):
            if taking:
                take(k - LAG, h)
            if giving:
                give(k, h)

    def exchange(t):
        @pl.when(t == 0)
        def _():
            gblk[pl.ds(col * slab, slab), :] = abuf[0]

        @pl.when(t > 0)
        def _():
            remote(
                abuf.at[t], gblk.at[pl.ds(col * slab, slab), :], a_send, a_recv,
                me, lax.rem(t + col, g),
            ).start()

    far = SKEW * (n - 1)
    lines = (
        (gp, zp, 0, zp_recv, ahead, me - 1, 1),
        (gm, zm, 1, zm_recv, behind, n - 1 - me, n - 1),
    )
    begin, ready = max(plan.sends - EARLY, LAG), plan.sends + LAG
    end = max(begin + far + g - LAG, ready + g)

    def along(line, q):
        _, zbuf, d, recv, to, _, _ = line
        return remote(zbuf.at[q], zbuf.at[q], z_send.at[d], recv.at[q], to, col)

    def first_block(line, q):
        return line[0][tab[plan.first + lax.rem(q + col, g)]].astype(F32)

    def chain(t):
        @pl.when(me != 0)
        def _():
            for line in lines:
                zbuf, hops, source = line[1], line[5], line[6]
                q = t - begin - SKEW * hops + LAG

                @pl.when((q >= LAG) & (q < g))
                def _():
                    @pl.when(me == source)
                    def _():
                        zbuf[q] = first_block(line, q).astype(BF16)

                    @pl.when(me != source)
                    def _():
                        along(line, q).wait_recv()
                        zbuf[q] = (zbuf[q].astype(F32) + first_block(line, q)).astype(BF16)

                    along(line, q).start()

        @pl.when((me == 0) & (t >= begin + far) & (t < begin + far + g - LAG))
        def _():
            q = t - begin - far + LAG
            for line, low in zip(lines, (0, half)):
                along(line, q).wait_recv()
                abuf[q, low:low + half, :] = (
                    line[1][q].astype(F32) + first_block(line, q)
                ).astype(BF16)
            exchange(q)

    def settle(t):
        i = t - ready

        @pl.when((i < g) & ((me != 0) | (i < LAG)))
        def _():
            r = jnp.where(me == 0, i, tab[plan.rank + lax.rem(i + col, g)])
            abuf[i, 0:half, :] = gp[nb + tab[sc + 2] + r]
            abuf[i, half:slab, :] = gm[nb + tab[sc + 5] - r]
            exchange(i)

    loop(0, LAG, lambda k: ring(k, taking=False))
    loop(LAG, begin, ring)
    loop(begin, plan.sends, lambda k: (ring(k), chain(k)))
    loop(plan.sends, ready, lambda k: (ring(k, giving=False), chain(k)))
    loop(ready, end, lambda k: (chain(k), settle(k)))

    remote(
        gblk.at[0:(g - 1) * slab], gblk.at[0:(g - 1) * slab], a_send, a_recv, me, col
    ).wait_recv()
    filled = tab[sc + 6] > 0
    tile = min(128, rows)

    def square(i, acc):
        x = gblk[pl.ds(pl.multiple_of(i * tile, tile), tile), :].astype(F32)
        return acc + jnp.sum(x * x, axis=0, keepdims=True)

    grad_square = jnp.sum(lax.fori_loop(0, rows // tile, square, jnp.zeros((1, cols), F32)))
    own_tile = jnp.full((8, 128), grad_square, F32)
    sq_own[...] = jnp.where(filled, own_tile, 0.0)
    sqz[me] = sq_own[...]
    for a in range(1, n):
        to = lax.rem(me + a, n)
        remote(sq_own, sqz.at[me], q_send.at[0], q_recv.at[0], to, col).start()
    for load in loads:
        load.wait()
    strip = 256

    def first_product(i, c):
        at = pl.ds(pl.multiple_of(i * strip, strip), strip)
        inner[:, at] = jnp.dot(lv[...], gblk[:, at], preferred_element_type=F32).astype(BF16)
        return c

    lax.fori_loop(0, cols // strip, first_product, 0)
    remote(sqz.at[0:n - 1], sqz.at[0:n - 1], q_send.at[0], q_recv.at[0], me, col).wait_recv()
    mid = sqz[0]
    for j in range(1, n):
        mid = mid + sqz[j]
    sq_mid[...] = mid
    sqs[col] = mid

    def tell(a):
        remote(
            sq_mid, sqs.at[col], q_send.at[1], q_recv.at[1], me, lax.rem(col + a, g)
        ).start()

    loop(1, g, tell)

    def second_product(i, acc):
        at = pl.ds(pl.multiple_of(i * strip, strip), strip)
        x = jnp.dot(inner[...], rv[:, at], preferred_element_type=F32)
        outer[:, at] = x
        return acc + jnp.sum(x * x, axis=0, keepdims=True)

    outer_square = jnp.sum(
        lax.fori_loop(0, cols // strip, second_product, jnp.zeros((1, strip), F32))
    )
    remote(sqs.at[0:g - 1], sqs.at[0:g - 1], q_send.at[1], q_recv.at[1], me, col).wait_recv()
    total = lax.fori_loop(0, g, lambda j, acc: acc + sqs[j], jnp.zeros((8, 128), F32))
    cells = float(rows * cols)
    outer_tile = jnp.full((8, 128), outer_square, F32)
    graft = (jnp.sqrt(own_tile / cells) * lax.rsqrt(outer_tile / cells + 1e-06))[0:1, :]
    clip = jnp.minimum(1.0, 0.5 * lax.rsqrt(total / (nb * cells) + 1e-06))[0:1, :]

    pairs = [(n // 2, 0)] + [(n // 2 - i, n // 2 + i) for i in range(1, n // 2)]
    def home(q, h, j, to):
        return remote(
            cbuf.at[2 * q + h, 0:plan.most[j]], fbuf.at[plan.base[j]:plan.base[j] + plan.most[j]],
            f_send.at[2 * q + h], f_recv.at[j], to, col,
        )

    def outward(q, pair):
        def part(i):
            at = pl.ds(pl.multiple_of(i * tile, tile), tile)
            for h, a in enumerate(pair):
                lanes = pl.ds(pl.multiple_of(lax.rem(me + a, n) * width, width), width)
                direction = jnp.where(filled, clip * (graft * outer[at, lanes]), 0.0)
                following = 0.9 * mv[at, lanes].astype(F32) + direction
                nm[at, lanes] = following.astype(BF16)
                ubuf[q, at, h * width:(h + 1) * width] = (
                    -0.8 * (0.9 * following + direction)
                ).astype(BF16)

        loop(0, rows // tile, part)
        rbufs[q][col] = ubuf[q, pl.ds(col * slab, slab), :]

        def back(a):
            to = lax.rem(col + a, g)
            remote(
                ubuf.at[q, pl.ds(to * slab, slab), :], rbufs[q].at[col],
                u_send.at[q], u_recv.at[q], me, to,
            ).start()

        loop(1, g, back)

    def homeward(q, pair):
        remote(
            rbufs[q].at[0:g - 1], rbufs[q].at[0:g - 1], u_send.at[q], u_recv.at[q], me, col
        ).wait_recv()

        def gather(r):
            piece = rbufs[q][tab[plan.slot + r]]
            cbuf[2 * q, r] = piece[:, 0:width]
            cbuf[2 * q + 1, r] = piece[:, width:2 * width]

        loop(0, g, gather)
        for j in range(n):
            @pl.when(me == j)
            def _():
                for h, a in enumerate(pair):
                    if a == 0:
                        fbuf[plan.base[j]:plan.base[j] + plan.most[j]] = (
                            cbuf[2 * q + h, 0:plan.most[j]]
                        )
                    else:
                        home(q, h, j, lax.rem(me + a, n)).start()

    for q, pair in enumerate(pairs):
        outward(q, pair)
        if q > 0:
            homeward(q - 1, pairs[q - 1])
    store = pltpu.make_async_copy(nm, new_momentum.at[0], load_sem.at[5])
    store.start()
    homeward(len(pairs) - 1, pairs[-1])

    for j in range(n):
        @pl.when(me != j)
        def _():
            home(0, 0, j, me).wait_recv()

    keep = pltpu.make_async_copy(fbuf, pieces, load_sem.at[0])
    keep.start()
    store.wait()
    keep.wait()
    for way in ways:
        remote(way[2], way[1], ring_send.at[way[3]], ring_recv.at[0, 0], me, col).wait_send()

    @pl.when(me != 0)
    def _():
        for line in lines:
            remote(
                line[1].at[LAG:g], line[1].at[LAG:g], z_send.at[line[2]], line[3].at[0], me, col
            ).wait_send()

    remote(abuf.at[1:g], abuf.at[1:g], a_send, a_recv, me, col).wait_send()
    remote(sqz.at[0:n - 1], sqz.at[0:n - 1], q_send.at[0], q_recv.at[0], me, col).wait_send()
    remote(sqs.at[0:g - 1], sqs.at[0:g - 1], q_send.at[1], q_recv.at[1], me, col).wait_send()
    for q, pair in enumerate(pairs):
        remote(
            rbufs[q].at[0:g - 1], rbufs[q].at[0:g - 1], u_send.at[q], u_recv.at[q], me, col
        ).wait_send()
        for j in range(n):
            @pl.when(me == j)
            def _():
                for h, a in enumerate(pair):
                    if a != 0:
                        home(q, h, j, me).wait_send()


def last_kernel(plan, pieces, following, tab, update, new_momentum, through, sems):
    step = plan.rows // 4
    rows = [slice(i * step, (i + 1) * step) for i in range(4)]
    reads = [
        pltpu.make_async_copy(following.at[0, r], through.at[r], sems.at[i])
        for i, r in enumerate(rows)
    ]
    writes = [
        pltpu.make_async_copy(through.at[r], new_momentum.at[0, r], sems.at[4 + i])
        for i, r in enumerate(rows)
    ]
    for read in reads:
        read.start()

    def place(b, c):
        update[b] = pieces[tab[plan.where + b]]
        return c

    lax.fori_loop(0, plan.blocks, place, 0)
    for read, write in zip(reads, writes):
        read.wait()
        write.start()
    for write in writes:
        write.wait()


def per_device(planes, groups, grads, left, right, momentum, block_order, owner_counts):
    blocks, slab, cols = grads.shape[1:]
    rows = left.shape[1]
    plan = Plan(planes, groups, blocks, rows, cols)
    half, width = slab // 2, cols // planes
    smem = pl.BlockSpec(memory_space=pltpu.SMEM)
    table = pl.pallas_call(
        functools.partial(table_kernel, plan),
        out_shape=jax.ShapeDtypeStruct((plan.size,), jnp.int32),
        in_specs=[smem, smem],
        out_specs=smem,
        scratch_shapes=[pltpu.SMEM((64,), jnp.int32)],
    )(block_order, owner_counts)
    anywhere = pl.BlockSpec(memory_space=pl.ANY)
    dma = pltpu.SemaphoreType.DMA
    held = plan.blocks + plan.sends
    pieces, following = pl.pallas_call(
        functools.partial(step_kernel, plan),
        out_shape=(
            jax.ShapeDtypeStruct((plan.slots, slab, width), BF16),
            jax.ShapeDtypeStruct((1, rows, cols), BF16),
        ),
        in_specs=[anywhere] * 4 + [smem],
        out_specs=(anywhere, anywhere),
        scratch_shapes=(
            [pltpu.VMEM((held, half, cols), BF16)] * 2
            + [pltpu.VMEM((plan.sends, half, cols), BF16)] * 4
            + [pltpu.VMEM((groups, half, cols), BF16)] * 2
            + [pltpu.VMEM((groups, slab, cols), BF16), pltpu.VMEM((rows, cols), BF16)]
            + [
                pltpu.VMEM((rows, rows), BF16),
                pltpu.VMEM((cols, cols), BF16),
                pltpu.VMEM((rows, cols), BF16),
                pltpu.VMEM((rows, cols), BF16),
                pltpu.VMEM((rows, cols), F32),
                pltpu.VMEM((rows, cols), BF16),
                pltpu.VMEM((planes // 2, rows, 2 * width), BF16),
                pltpu.VMEM((planes, groups, slab, width), BF16),
                pltpu.VMEM((plan.slots, slab, width), BF16),
                pltpu.VMEM((8, 128), F32),
                pltpu.VMEM((8, 128), F32),
                pltpu.VMEM((planes, 8, 128), F32),
                pltpu.VMEM((groups, 8, 128), F32),
            ]
            + [
                dma((6,)),
                dma((2,)),
                dma((2 * PARTS, plan.sends)),
                dma((2,)),
                dma((groups,)),
                dma((groups,)),
                dma,
                dma,
                dma((2,)),
                dma((2,)),
                dma((planes // 2,)),
                dma((planes // 2,)),
                dma((planes,)),
                dma((planes,)),
            ]
            + [pltpu.VMEM((groups, slab, 2 * width), BF16)] * (planes // 2)
        ),
        compiler_params=pltpu.CompilerParams(
            collective_id=0, has_side_effects=True, vmem_limit_bytes=56 * 1024 * 1024
        ),
        cost_estimate=pl.CostEstimate(
            flops=2 * rows * cols * (rows + cols), bytes_accessed=2 * 13 * rows * cols // 2,
            transcendentals=0,
        ),
    )(grads, left, right, momentum, table)
    return pl.pallas_call(
        functools.partial(last_kernel, plan),
        out_shape=(
            jax.ShapeDtypeStruct((blocks, slab, width), BF16),
            jax.ShapeDtypeStruct((1, rows, cols), BF16),
        ),
        in_specs=[pl.BlockSpec(memory_space=pltpu.VMEM), anywhere, smem],
        out_specs=(pl.BlockSpec(memory_space=pltpu.VMEM), anywhere),
        scratch_shapes=[pltpu.VMEM((rows, cols), BF16), dma((8,))],
    )(pieces, following, table)


def solution(mesh):
    slots = P(("dp", "shard"), None, None)
    return jax.shard_map(
        functools.partial(per_device, mesh.shape["dp"], mesh.shape["shard"]),
        mesh=mesh,
        in_specs=(P("dp", None, "shard", None), slots, slots, slots, P(), P()),
        out_specs=(P(None, "shard", "dp"), slots),
        check_vma=False,
    )
```

```python
import functools

import jax
import jax.numpy as jnp
from jax import lax
from jax.experimental import pallas as pl
from jax.experimental.pallas import tpu as pltpu
from jax.sharding import PartitionSpec as P

MESH = pl.DeviceIdType.MESH
LAG = 3
PARTS = 1
SKEW = 4
EARLY = 20
F32 = jnp.float32
BF16 = jnp.bfloat16


class Plan:
    def __init__(self, planes, groups, blocks, rows, cols):
        self.planes, self.groups, self.blocks = planes, groups, blocks
        self.rows, self.cols = rows, cols
        extras = blocks - groups
        self.most = [groups] + [
            min(groups, (extras - (planes - 1 - j)) // j) for j in range(1, planes)
        ]
        self.base = [sum(self.most[:j]) for j in range(planes)]
        self.slots = sum(self.most)
        self.sends = max(extras - (planes - 2), LAG) + (planes - 2) * LAG
        place = 0
        for name, size in (
            ("before", self.sends),
            ("order", 2 * (self.sends + LAG)),
            ("first", groups),
            ("rank", groups),
            ("slot", groups),
            ("where", blocks),
            ("scalars", 16),
        ):
            setattr(self, name, place)
            place += size
        self.size = place


def chunks_of(n):
    return [(n // 2,)] + [(n // 2 - i, n // 2 + i) for i in range(1, n // 2)] + [(0,)]


def table_kernel(plan, order_ref, counts_ref, tab, held):
    n, g = plan.planes, plan.groups
    me, col = lax.axis_index("dp"), lax.axis_index("shard")
    prev, nxt = lax.rem(me + n - 1, n), lax.rem(me + 1, n)
    hist, start, rank, width = 0, 16, 32, 48
    for i in range(plan.first):
        tab[i] = 0
    for i in range(16):
        held[hist + i] = 0
        held[rank + i] = 0

    def tally(o, seen):
        p, mine = seen
        k = counts_ref[o]
        held[hist + k] = held[hist + k] + 1
        b = order_ref[p]
        tab[plan.first + o] = b
        tab[plan.where + b] = o
        tab[plan.rank + o] = jnp.where(k > me, mine, 0)
        tab[plan.slot + o] = 0
        tab[plan.slot + mine] = o
        return p + k, mine + jnp.where(k > me, 1, 0)

    lax.fori_loop(0, g, tally, (jnp.int32(0), jnp.int32(0)))
    run = jnp.int32(0)
    at = jnp.int32(0)
    for j in range(n - 1, -1, -1):
        run = run + held[hist + j + 1]
        wide = jnp.int32(LAG) if j == 0 else jnp.maximum(run, LAG)
        held[start + j] = at
        held[width + j] = wide
        at = at + wide
    total = at
    for r in range(LAG):
        b = tab[plan.first + lax.rem(col + r, g)]
        tab[plan.order + held[start] + r] = b
        tab[plan.order + held[start] + r + total] = b

    def group(o, p):
        count = counts_ref[o]

        def one(j, c):
            b = order_ref[p + j]
            r = held[rank + j]
            held[rank + j] = r + 1
            u = plan.order + held[start + j] + r
            tab[u] = b
            tab[u + total] = b
            offset = jnp.int32(plan.base[1])
            for i in range(2, n):
                offset = jnp.where(j >= i, plan.base[i], offset)
            tab[plan.where + b] = offset + r
            return c

        lax.fori_loop(1, count, one, 0)
        return p + count

    lax.fori_loop(0, g, group, jnp.int32(0))
    s = plan.scalars
    before, after, own = held[width + prev], held[width + nxt], held[width + me]
    tab[s + 0] = plan.order + held[start + prev]
    tab[s + 1] = before
    tab[s + 2] = total - before - own
    tab[s + 3] = plan.order + held[start + nxt] + after - 1 + total
    tab[s + 4] = after
    tab[s + 5] = total - after - 1
    tab[s + 6] = jnp.where(counts_ref[col] > me, 1, 0)


def step_kernel(
    plan,
    grads, left, right, momentum, tab,
    pieces, new_momentum,
    gp, gm, landp, landm, outp, outm, zp, zm, abuf, gblk,
    lv, rv, mv, inner, outer, nm, ubuf, cbuf, fbuf,
    sq_own, sq_mid, sqz, sqs,
    load_sem, ring_send, ring_recv, z_send, zp_recv, zm_recv, a_send, a_recv,
    q_send, q_recv, u_send, u_recv, f_send, f_recv,
    *rbufs,
):
    n, g, nb = plan.planes, plan.groups, plan.blocks
    rows, cols = plan.rows, plan.cols
    slab = rows // g
    half = slab // 2
    width = cols // n
    me, col = lax.axis_index("dp"), lax.axis_index("shard")
    ahead, behind = lax.rem(me + 1, n), lax.rem(me + n - 1, n)

    def loop(low, high, body):
        lax.fori_loop(low, high, lambda i, c: (body(i), c)[1], 0)

    def remote(src, dst, send, recv, dp, shard):
        return pltpu.make_async_remote_copy(
            src_ref=src, dst_ref=dst, send_sem=send, recv_sem=recv,
            device_id={"dp": dp, "shard": shard}, device_id_type=MESH,
        )

    load_p = pltpu.make_async_copy(grads.at[0, :, 0:half, :], gp.at[0:nb], load_sem.at[0])
    load_m = pltpu.make_async_copy(grads.at[0, :, half:slab, :], gm.at[0:nb], load_sem.at[1])
    load_p.start()
    load_m.start()
    loads = [
        pltpu.make_async_copy(src.at[0], dst, load_sem.at[2 + i])
        for i, (src, dst) in enumerate(((left, lv), (right, rv), (momentum, mv)))
    ]

    barrier = pltpu.get_barrier_semaphore()
    for a in range(1, n):
        pl.semaphore_signal(
            barrier, inc=1, device_id={"dp": lax.rem(me + a, n), "shard": col}, device_id_type=MESH
        )

    def greet(a):
        pl.semaphore_signal(
            barrier, inc=1, device_id={"dp": me, "shard": lax.rem(col + a, g)}, device_id_type=MESH
        )

    loop(1, g, greet)
    pl.semaphore_wait(barrier, n - 1 + g - 1)
    load_p.wait()
    load_m.wait()
    for load in loads:
        load.start()

    sc = plan.scalars
    ways = (
        (gp, landp, outp, 0, ahead, tab[sc], 1, tab[sc + 1]),
        (gm, landm, outm, 1, behind, tab[sc + 3], -1, tab[sc + 4]),
    )
    parts = tuple(slice(h * (cols // PARTS), (h + 1) * (cols // PARTS)) for h in range(PARTS))

    def passing(way, k, h):
        _, land, out, d, to, _, _, _ = way
        return remote(
            out.at[k, :, parts[h]], land.at[k, :, parts[h]],
            ring_send.at[d], ring_recv.at[PARTS * d + h, k], to, col,
        )

    def take(k, h):
        for way in ways:
            held, land, _, _, _, start, sign, lag = way
            passing(way, k, h).wait_recv()
            own = held[tab[jnp.maximum(start + sign * (lag + k), 0)], :, parts[h]]
            held[nb + k, :, parts[h]] = (
                land[k, :, parts[h]].astype(F32) + own.astype(F32)
            ).astype(BF16)

    def give(k, h):
        for way in ways:
            held, _, out, _, _, start, sign, lag = way
            source = jnp.where(k < lag, tab[jnp.maximum(start + sign * k, 0)], nb + k - lag)
            out[k, :, parts[h]] = held[source, :, parts[h]]
            passing(way, k, h).start()

    def ring(k, taking=True, giving=True):
        for h in range(PARTS):
            if taking:
                take(k - LAG, h)
            if giving:
                give(k, h)

    def exchange(t):
        @pl.when(t == 0)
        def _():
            gblk[pl.ds(col * slab, slab), :] = abuf[0]

        @pl.when(t > 0)
        def _():
            remote(
                abuf.at[t], gblk.at[pl.ds(col * slab, slab), :], a_send, a_recv,
                me, lax.rem(t + col, g),
            ).start()

    far = SKEW * (n - 1)
    lines = (
        (gp, zp, 0, zp_recv, ahead, me - 1, 1),
        (gm, zm, 1, zm_recv, behind, n - 1 - me, n - 1),
    )
    begin, ready = max(plan.sends - EARLY, LAG), plan.sends + LAG
    end = max(begin + far + g - LAG, ready + g)

    def along(line, q):
        _, zbuf, d, recv, to, _, _ = line
        return remote(zbuf.at[q], zbuf.at[q], z_send.at[d], recv.at[q], to, col)

    def first_block(line, q):
        return line[0][tab[plan.first + lax.rem(q + col, g)]].astype(F32)

    def chain(t):
        @pl.when(me != 0)
        def _():
            for line in lines:
                zbuf, hops, source = line[1], line[5], line[6]
                q = t - begin - SKEW * hops + LAG

                @pl.when((q >= LAG) & (q < g))
                def _():
                    @pl.when(me == source)
                    def _():
                        zbuf[q] = first_block(line, q).astype(BF16)

                    @pl.when(me != source)
                    def _():
                        along(line, q).wait_recv()
                        zbuf[q] = (zbuf[q].astype(F32) + first_block(line, q)).astype(BF16)

                    along(line, q).start()

        @pl.when((me == 0) & (t >= begin + far) & (t < begin + far + g - LAG))
        def _():
            q = t - begin - far + LAG
            for line, low in zip(lines, (0, half)):
                along(line, q).wait_recv()
                abuf[q, low:low + half, :] = (
                    line[1][q].astype(F32) + first_block(line, q)
                ).astype(BF16)
            exchange(q)

    def settle(t):
        i = t - ready

        @pl.when((i < g) & ((me != 0) | (i < LAG)))
        def _():
            r = jnp.where(me == 0, i, tab[plan.rank + lax.rem(i + col, g)])
            abuf[i, 0:half, :] = gp[nb + tab[sc + 2] + r]
            abuf[i, half:slab, :] = gm[nb + tab[sc + 5] - r]
            exchange(i)

    loop(0, LAG, lambda k: ring(k, taking=False))
    loop(LAG, begin, ring)
    loop(begin, plan.sends, lambda k: (ring(k), chain(k)))
    loop(plan.sends, ready, lambda k: (ring(k, giving=False), chain(k)))
    loop(ready, end, lambda k: (chain(k), settle(k)))

    remote(
        gblk.at[0:(g - 1) * slab], gblk.at[0:(g - 1) * slab], a_send, a_recv, me, col
    ).wait_recv()
    filled = tab[sc + 6] > 0
    tile = min(128, rows)

    def square(i, acc):
        x = gblk[pl.ds(pl.multiple_of(i * tile, tile), tile), :].astype(F32)
        return acc + jnp.sum(x * x, axis=0, keepdims=True)

    grad_square = jnp.sum(lax.fori_loop(0, rows // tile, square, jnp.zeros((1, cols), F32)))
    own_tile = jnp.full((8, 128), grad_square, F32)
    sq_own[...] = jnp.where(filled, own_tile, 0.0)
    sqz[me] = sq_own[...]
    for a in range(1, n):
        to = lax.rem(me + a, n)
        remote(sq_own, sqz.at[me], q_send.at[0], q_recv.at[0], to, col).start()
    for load in loads:
        load.wait()
    strip = 256

    def first_product(i, c):
        at = pl.ds(pl.multiple_of(i * strip, strip), strip)
        inner[:, at] = jnp.dot(lv[...], gblk[:, at], preferred_element_type=F32).astype(BF16)
        return c

    lax.fori_loop(0, cols // strip, first_product, 0)
    remote(sqz.at[0:n - 1], sqz.at[0:n - 1], q_send.at[0], q_recv.at[0], me, col).wait_recv()
    mid = sqz[0]
    for j in range(1, n):
        mid = mid + sqz[j]
    sq_mid[...] = mid
    sqs[col] = mid

    def tell(a):
        remote(
            sq_mid, sqs.at[col], q_send.at[1], q_recv.at[1], me, lax.rem(col + a, g)
        ).start()

    loop(1, g, tell)

    def second_product(i, acc):
        at = pl.ds(pl.multiple_of(i * strip, strip), strip)
        x = jnp.dot(inner[...], rv[:, at], preferred_element_type=F32)
        outer[:, at] = x
        return acc + jnp.sum(x * x, axis=0, keepdims=True)

    outer_square = jnp.sum(
        lax.fori_loop(0, cols // strip, second_product, jnp.zeros((1, strip), F32))
    )
    remote(sqs.at[0:g - 1], sqs.at[0:g - 1], q_send.at[1], q_recv.at[1], me, col).wait_recv()
    total = lax.fori_loop(0, g, lambda j, acc: acc + sqs[j], jnp.zeros((8, 128), F32))
    cells = float(rows * cols)
    outer_tile = jnp.full((8, 128), outer_square, F32)
    graft = (jnp.sqrt(own_tile / cells) * lax.rsqrt(outer_tile / cells + 1e-06))[0:1, :]
    clip = jnp.minimum(1.0, 0.5 * lax.rsqrt(total / (nb * cells) + 1e-06))[0:1, :]

    pairs = chunks_of(n)
    def home(a, j, to):
        return remote(
            cbuf.at[a, 0:plan.most[j]], fbuf.at[plan.base[j]:plan.base[j] + plan.most[j]],
            f_send.at[a], f_recv.at[j], to, col,
        )

    def outward(q, pair):
        def part(i):
            at = pl.ds(pl.multiple_of(i * tile, tile), tile)
            for h, a in enumerate(pair):
                lanes = pl.ds(pl.multiple_of(lax.rem(me + a, n) * width, width), width)
                direction = jnp.where(filled, clip * (graft * outer[at, lanes]), 0.0)
                following = 0.9 * mv[at, lanes].astype(F32) + direction
                nm[at, lanes] = following.astype(BF16)
                ubuf[q, at, h * width:(h + 1) * width] = (
                    -0.8 * (0.9 * following + direction)
                ).astype(BF16)

        loop(0, rows // tile, part)
        rbufs[q][col] = ubuf[q, pl.ds(col * slab, slab), 0:len(pair) * width]

        def back(a):
            to = lax.rem(col + a, g)
            remote(
                ubuf.at[q, pl.ds(to * slab, slab), 0:len(pair) * width], rbufs[q].at[col],
                u_send.at[q], u_recv.at[q], me, to,
            ).start()

        loop(1, g, back)

    def homeward(q, pair):
        remote(
            rbufs[q].at[0:g - 1], rbufs[q].at[0:g - 1], u_send.at[q], u_recv.at[q], me, col
        ).wait_recv()

        def gather(r):
            piece = rbufs[q][tab[plan.slot + r]]
            for h, a in enumerate(pair):
                cbuf[a, r] = piece[:, h * width:(h + 1) * width]

        loop(0, g, gather)
        for j in range(n):
            @pl.when(me == j)
            def _():
                for a in pair:
                    if a == 0:
                        fbuf[plan.base[j]:plan.base[j] + plan.most[j]] = (
                            cbuf[a, 0:plan.most[j]]
                        )
                    else:
                        home(a, j, lax.rem(me + a, n)).start()

    for q, pair in enumerate(pairs):
        outward(q, pair)
        if q > 0:
            homeward(q - 1, pairs[q - 1])
    store = pltpu.make_async_copy(nm, new_momentum.at[0], load_sem.at[5])
    store.start()
    homeward(len(pairs) - 1, pairs[-1])

    for j in range(n):
        @pl.when(me != j)
        def _():
            home(0, j, me).wait_recv()

    keep = pltpu.make_async_copy(fbuf, pieces, load_sem.at[0])
    keep.start()
    store.wait()
    keep.wait()
    for way in ways:
        remote(way[2], way[1], ring_send.at[way[3]], ring_recv.at[0, 0], me, col).wait_send()

    @pl.when(me != 0)
    def _():
        for line in lines:
            remote(
                line[1].at[LAG:g], line[1].at[LAG:g], z_send.at[line[2]], line[3].at[0], me, col
            ).wait_send()

    remote(abuf.at[1:g], abuf.at[1:g], a_send, a_recv, me, col).wait_send()
    remote(sqz.at[0:n - 1], sqz.at[0:n - 1], q_send.at[0], q_recv.at[0], me, col).wait_send()
    remote(sqs.at[0:g - 1], sqs.at[0:g - 1], q_send.at[1], q_recv.at[1], me, col).wait_send()
    for q, pair in enumerate(pairs):
        remote(
            rbufs[q].at[0:g - 1], rbufs[q].at[0:g - 1], u_send.at[q], u_recv.at[q], me, col
        ).wait_send()
        for j in range(n):
            @pl.when(me == j)
            def _():
                for a in pair:
                    if a != 0:
                        home(a, j, me).wait_send()


def last_kernel(plan, pieces, following, tab, update, new_momentum, through, held, placed, sems):
    step = plan.rows // 4
    rows = [slice(i * step, (i + 1) * step) for i in range(4)]
    fetch = pltpu.make_async_copy(pieces, held, sems.at[8])
    reads = [
        pltpu.make_async_copy(following.at[0, r], through.at[r], sems.at[i])
        for i, r in enumerate(rows)
    ]
    writes = [
        pltpu.make_async_copy(through.at[r], new_momentum.at[0, r], sems.at[4 + i])
        for i, r in enumerate(rows)
    ]
    fetch.start()
    for read in reads:
        read.start()
    fetch.wait()

    def place(b, c):
        placed[b] = held[tab[plan.where + b]]
        return c

    lax.fori_loop(0, plan.blocks, place, 0)
    put = pltpu.make_async_copy(placed, update, sems.at[9])
    put.start()
    for read, write in zip(reads, writes):
        read.wait()
        write.start()
    for write in writes:
        write.wait()
    put.wait()


def per_device(planes, groups, grads, left, right, momentum, block_order, owner_counts):
    blocks, slab, cols = grads.shape[1:]
    rows = left.shape[1]
    plan = Plan(planes, groups, blocks, rows, cols)
    half, width = slab // 2, cols // planes
    smem = pl.BlockSpec(memory_space=pltpu.SMEM)
    table = pl.pallas_call(
        functools.partial(table_kernel, plan),
        out_shape=jax.ShapeDtypeStruct((plan.size,), jnp.int32),
        in_specs=[smem, smem],
        out_specs=smem,
        scratch_shapes=[pltpu.SMEM((64,), jnp.int32)],
    )(block_order, owner_counts)
    anywhere = pl.BlockSpec(memory_space=pl.ANY)
    dma = pltpu.SemaphoreType.DMA
    held = plan.blocks + plan.sends
    chunks = chunks_of(planes)
    pieces, following = pl.pallas_call(
        functools.partial(step_kernel, plan),
        out_shape=(
            jax.ShapeDtypeStruct((plan.slots, slab, width), BF16),
            jax.ShapeDtypeStruct((1, rows, cols), BF16),
        ),
        in_specs=[anywhere] * 4 + [smem],
        out_specs=(anywhere, anywhere),
        scratch_shapes=(
            [pltpu.VMEM((held, half, cols), BF16)] * 2
            + [pltpu.VMEM((plan.sends, half, cols), BF16)] * 4
            + [pltpu.VMEM((groups, half, cols), BF16)] * 2
            + [pltpu.VMEM((groups, slab, cols), BF16), pltpu.VMEM((rows, cols), BF16)]
            + [
                pltpu.VMEM((rows, rows), BF16),
                pltpu.VMEM((cols, cols), BF16),
                pltpu.VMEM((rows, cols), BF16),
                pltpu.VMEM((rows, cols), BF16),
                pltpu.VMEM((rows, cols), F32),
                pltpu.VMEM((rows, cols), BF16),
                pltpu.VMEM((len(chunks), rows, 2 * width), BF16),
                pltpu.VMEM((planes, groups, slab, width), BF16),
                pltpu.VMEM((plan.slots, slab, width), BF16),
                pltpu.VMEM((8, 128), F32),
                pltpu.VMEM((8, 128), F32),
                pltpu.VMEM((planes, 8, 128), F32),
                pltpu.VMEM((groups, 8, 128), F32),
            ]
            + [
                dma((6,)),
                dma((2,)),
                dma((2 * PARTS, plan.sends)),
                dma((2,)),
                dma((groups,)),
                dma((groups,)),
                dma,
                dma,
                dma((2,)),
                dma((2,)),
                dma((len(chunks),)),
                dma((len(chunks),)),
                dma((planes,)),
                dma((planes,)),
            ]
            + [pltpu.VMEM((groups, slab, len(c) * width), BF16) for c in chunks]
        ),
        compiler_params=pltpu.CompilerParams(
            collective_id=0, has_side_effects=True, vmem_limit_bytes=56 * 1024 * 1024
        ),
        cost_estimate=pl.CostEstimate(
            flops=2 * rows * cols * (rows + cols), bytes_accessed=2 * 13 * rows * cols // 2,
            transcendentals=0,
        ),
    )(grads, left, right, momentum, table)
    return pl.pallas_call(
        functools.partial(last_kernel, plan),
        out_shape=(
            jax.ShapeDtypeStruct((blocks, slab, width), BF16),
            jax.ShapeDtypeStruct((1, rows, cols), BF16),
        ),
        in_specs=[anywhere, anywhere, smem],
        out_specs=(anywhere, anywhere),
        scratch_shapes=[
            pltpu.VMEM((rows, cols), BF16),
            pltpu.VMEM((plan.slots, slab, width), BF16),
            pltpu.VMEM((blocks, slab, width), BF16),
            dma((10,)),
        ],
    )(pieces, following, table)


def solution(mesh):
    slots = P(("dp", "shard"), None, None)
    return jax.shard_map(
        functools.partial(per_device, mesh.shape["dp"], mesh.shape["shard"]),
        mesh=mesh,
        in_specs=(P("dp", None, "shard", None), slots, slots, slots, P(), P()),
        out_specs=(P(None, "shard", "dp"), slots),
        check_vma=False,
    )
```

```python
import functools

import jax
import jax.numpy as jnp
from jax import lax
from jax.experimental import pallas as pl
from jax.experimental.pallas import tpu as pltpu
from jax.sharding import PartitionSpec as P

MESH = pl.DeviceIdType.MESH
LAG = 3
PARTS = 1
SKEW = 3
EARLY = 18
F32 = jnp.float32
BF16 = jnp.bfloat16


class Plan:
    def __init__(self, planes, groups, blocks, rows, cols):
        self.planes, self.groups, self.blocks = planes, groups, blocks
        self.rows, self.cols = rows, cols
        extras = blocks - groups
        self.most = [groups] + [
            min(groups, (extras - (planes - 1 - j)) // j) for j in range(1, planes)
        ]
        self.base = [sum(self.most[:j]) for j in range(planes)]
        self.slots = sum(self.most)
        self.sends = max(extras - (planes - 2), LAG) + (planes - 2) * LAG
        place = 0
        for name, size in (
            ("before", self.sends),
            ("order", 2 * (self.sends + LAG)),
            ("first", groups),
            ("rank", groups),
            ("slot", groups),
            ("where", blocks),
            ("scalars", 16),
        ):
            setattr(self, name, place)
            place += size
        self.size = place


def chunks_of(n):
    return [(n // 2,)] + [(n // 2 - i, n // 2 + i) for i in range(1, n // 2)] + [(0,)]


def table_kernel(plan, order_ref, counts_ref, tab, held):
    n, g = plan.planes, plan.groups
    me, col = lax.axis_index("dp"), lax.axis_index("shard")
    prev, nxt = lax.rem(me + n - 1, n), lax.rem(me + 1, n)
    hist, start, rank, width = 0, 16, 32, 48
    for i in range(plan.first):
        tab[i] = 0
    for i in range(16):
        held[hist + i] = 0
        held[rank + i] = 0

    def tally(o, seen):
        p, mine = seen
        k = counts_ref[o]
        held[hist + k] = held[hist + k] + 1
        b = order_ref[p]
        tab[plan.first + o] = b
        tab[plan.where + b] = o
        tab[plan.rank + o] = jnp.where(k > me, mine, 0)
        tab[plan.slot + o] = 0
        tab[plan.slot + mine] = o
        return p + k, mine + jnp.where(k > me, 1, 0)

    lax.fori_loop(0, g, tally, (jnp.int32(0), jnp.int32(0)))
    run = jnp.int32(0)
    at = jnp.int32(0)
    for j in range(n - 1, -1, -1):
        run = run + held[hist + j + 1]
        wide = jnp.int32(LAG) if j == 0 else jnp.maximum(run, LAG)
        held[start + j] = at
        held[width + j] = wide
        at = at + wide
    total = at
    for r in range(LAG):
        b = tab[plan.first + lax.rem(col + r, g)]
        tab[plan.order + held[start] + r] = b
        tab[plan.order + held[start] + r + total] = b

    def group(o, p):
        count = counts_ref[o]

        def one(j, c):
            b = order_ref[p + j]
            r = held[rank + j]
            held[rank + j] = r + 1
            u = plan.order + held[start + j] + r
            tab[u] = b
            tab[u + total] = b
            offset = jnp.int32(plan.base[1])
            for i in range(2, n):
                offset = jnp.where(j >= i, plan.base[i], offset)
            tab[plan.where + b] = offset + r
            return c

        lax.fori_loop(1, count, one, 0)
        return p + count

    lax.fori_loop(0, g, group, jnp.int32(0))
    s = plan.scalars
    before, after, own = held[width + prev], held[width + nxt], held[width + me]
    tab[s + 0] = plan.order + held[start + prev]
    tab[s + 1] = before
    tab[s + 2] = total - before - own
    tab[s + 3] = plan.order + held[start + nxt] + after - 1 + total
    tab[s + 4] = after
    tab[s + 5] = total - after - 1
    tab[s + 6] = jnp.where(counts_ref[col] > me, 1, 0)


def step_kernel(
    plan,
    grads, left, right, momentum, tab,
    pieces, new_momentum,
    gp, gm, landp, landm, outp, outm, zp, zm, abuf, gblk,
    lv, rv, mv, inner, outer, nm, ubuf, cbuf, fbuf,
    sq_own, sq_mid, sqz, sqs,
    load_sem, ring_send, ring_recv, z_send, zp_recv, zm_recv, a_send, a_recv,
    q_send, q_recv, u_send, u_recv, f_send, f_recv,
    direct, zland, h_send, h_recv, g_send, g_recv,
    *rbufs,
):
    n, g, nb = plan.planes, plan.groups, plan.blocks
    rows, cols = plan.rows, plan.cols
    slab = rows // g
    half = slab // 2
    width = cols // n
    me, col = lax.axis_index("dp"), lax.axis_index("shard")
    ahead, behind = lax.rem(me + 1, n), lax.rem(me + n - 1, n)

    def loop(low, high, body):
        lax.fori_loop(low, high, lambda i, c: (body(i), c)[1], 0)

    def remote(src, dst, send, recv, dp, shard):
        return pltpu.make_async_remote_copy(
            src_ref=src, dst_ref=dst, send_sem=send, recv_sem=recv,
            device_id={"dp": dp, "shard": shard}, device_id_type=MESH,
        )

    load_p = pltpu.make_async_copy(grads.at[0, :, 0:half, :], gp.at[0:nb], load_sem.at[0])
    load_m = pltpu.make_async_copy(grads.at[0, :, half:slab, :], gm.at[0:nb], load_sem.at[1])
    load_p.start()
    load_m.start()
    loads = [
        pltpu.make_async_copy(src.at[0], dst, load_sem.at[2 + i])
        for i, (src, dst) in enumerate(((left, lv), (right, rv), (momentum, mv)))
    ]

    barrier = pltpu.get_barrier_semaphore()
    for a in range(1, n):
        pl.semaphore_signal(
            barrier, inc=1, device_id={"dp": lax.rem(me + a, n), "shard": col}, device_id_type=MESH
        )

    def greet(a):
        pl.semaphore_signal(
            barrier, inc=1, device_id={"dp": me, "shard": lax.rem(col + a, g)}, device_id_type=MESH
        )

    loop(1, g, greet)
    pl.semaphore_wait(barrier, n - 1 + g - 1)
    load_p.wait()
    load_m.wait()
    for load in loads:
        load.start()

    sc = plan.scalars
    ways = (
        (gp, landp, outp, 0, ahead, tab[sc], 1, tab[sc + 1]),
        (gm, landm, outm, 1, behind, tab[sc + 3], -1, tab[sc + 4]),
    )
    parts = tuple(slice(h * (cols // PARTS), (h + 1) * (cols // PARTS)) for h in range(PARTS))

    def passing(way, k, h):
        _, land, out, d, to, _, _, _ = way
        return remote(
            out.at[k, :, parts[h]], land.at[k, :, parts[h]],
            ring_send.at[d], ring_recv.at[PARTS * d + h, k], to, col,
        )

    def take(k, h):
        for way in ways:
            held, land, _, _, _, start, sign, lag = way
            passing(way, k, h).wait_recv()
            own = held[tab[jnp.maximum(start + sign * (lag + k), 0)], :, parts[h]]
            held[nb + k, :, parts[h]] = (
                land[k, :, parts[h]].astype(F32) + own.astype(F32)
            ).astype(BF16)

    def give(k, h):
        for way in ways:
            held, _, out, _, _, start, sign, lag = way
            source = jnp.where(k < lag, tab[jnp.maximum(start + sign * k, 0)], nb + k - lag)
            out[k, :, parts[h]] = held[source, :, parts[h]]
            passing(way, k, h).start()

    def ring(k, taking=True, giving=True):
        for h in range(PARTS):
            if taking:
                take(k - LAG, h)
            if giving:
                give(k, h)

    def exchange(t):
        @pl.when(t == 0)
        def _():
            gblk[pl.ds(col * slab, slab), :] = abuf[0]

        @pl.when(t > 0)
        def _():
            remote(
                abuf.at[t], gblk.at[pl.ds(col * slab, slab), :], a_send, a_recv,
                me, lax.rem(t + col, g),
            ).start()

    far = SKEW * (n - 1)
    lines = (
        (gp, zp, 0, zp_recv, ahead, me - 1, 1),
        (gm, zm, 1, zm_recv, behind, n - 1 - me, n - 1),
    )
    begin, ready = max(plan.sends - EARLY, LAG), plan.sends + LAG
    end = max(begin + far + g - LAG, ready + g)

    def along(line, q):
        _, zbuf, d, recv, to, _, _ = line
        return remote(zbuf.at[q], zbuf.at[q], z_send.at[d], recv.at[q], to, col)

    def first_block(line, q):
        return line[0][tab[plan.first + lax.rem(q + col, g)]].astype(F32)

    def chain(t):
        @pl.when(me != 0)
        def _():
            for line in lines:
                zbuf, hops, source = line[1], line[5], line[6]
                q = t - begin - SKEW * hops + LAG

                @pl.when((q >= LAG) & (q < g))
                def _():
                    @pl.when(me == source)
                    def _():
                        zbuf[q] = first_block(line, q).astype(BF16)

                    @pl.when(me != source)
                    def _():
                        along(line, q).wait_recv()
                        zbuf[q] = (zbuf[q].astype(F32) + first_block(line, q)).astype(BF16)

                    along(line, q).start()

        @pl.when((me == 0) & (t >= begin + far) & (t < begin + far + g - LAG))
        def _():
            q = t - begin - far + LAG
            for line, low in zip(lines, (0, half)):
                along(line, q).wait_recv()
                abuf[q, low:low + half, :] = (
                    line[1][q].astype(F32) + first_block(line, q)
                ).astype(BF16)
            exchange(q)

    def settle(t):
        i = t - ready

        @pl.when((i < g) & ((me != 0) | (i < LAG)))
        def _():
            r = jnp.where(me == 0, i, tab[plan.rank + lax.rem(i + col, g)])
            abuf[i, 0:half, :] = gp[nb + tab[sc + 2] + r]
            abuf[i, half:slab, :] = gm[nb + tab[sc + 5] - r]
            exchange(i)

    loop(0, LAG, lambda k: ring(k, taking=False))
    loop(LAG, begin, ring)
    loop(begin, plan.sends, lambda k: (ring(k), chain(k)))
    loop(plan.sends, ready, lambda k: (ring(k, giving=False), chain(k)))
    loop(ready, end, lambda k: (chain(k), settle(k)))

    remote(
        gblk.at[0:(g - 1) * slab], gblk.at[0:(g - 1) * slab], a_send, a_recv, me, col
    ).wait_recv()
    filled = tab[sc + 6] > 0
    tile = min(128, rows)

    def square(i, acc):
        x = gblk[pl.ds(pl.multiple_of(i * tile, tile), tile), :].astype(F32)
        return acc + jnp.sum(x * x, axis=0, keepdims=True)

    grad_square = jnp.sum(lax.fori_loop(0, rows // tile, square, jnp.zeros((1, cols), F32)))
    own_tile = jnp.full((8, 128), grad_square, F32)
    sq_own[...] = jnp.where(filled, own_tile, 0.0)
    sqz[me] = sq_own[...]
    for a in range(1, n):
        to = lax.rem(me + a, n)
        remote(sq_own, sqz.at[me], q_send.at[0], q_recv.at[0], to, col).start()
    for load in loads:
        load.wait()
    strip = 256

    def first_product(i, c):
        at = pl.ds(pl.multiple_of(i * strip, strip), strip)
        inner[:, at] = jnp.dot(lv[...], gblk[:, at], preferred_element_type=F32).astype(BF16)
        return c

    lax.fori_loop(0, cols // strip, first_product, 0)
    remote(sqz.at[0:n - 1], sqz.at[0:n - 1], q_send.at[0], q_recv.at[0], me, col).wait_recv()
    mid = sqz[0]
    for j in range(1, n):
        mid = mid + sqz[j]
    sq_mid[...] = mid
    sqs[col] = mid

    def tell(a):
        remote(
            sq_mid, sqs.at[col], q_send.at[1], q_recv.at[1], me, lax.rem(col + a, g)
        ).start()

    loop(1, g, tell)

    def second_product(i, acc):
        at = pl.ds(pl.multiple_of(i * strip, strip), strip)
        x = jnp.dot(inner[...], rv[:, at], preferred_element_type=F32)
        outer[:, at] = x
        return acc + jnp.sum(x * x, axis=0, keepdims=True)

    outer_square = jnp.sum(
        lax.fori_loop(0, cols // strip, second_product, jnp.zeros((1, strip), F32))
    )
    remote(sqs.at[0:g - 1], sqs.at[0:g - 1], q_send.at[1], q_recv.at[1], me, col).wait_recv()
    total = lax.fori_loop(0, g, lambda j, acc: acc + sqs[j], jnp.zeros((8, 128), F32))
    cells = float(rows * cols)
    outer_tile = jnp.full((8, 128), outer_square, F32)
    graft = (jnp.sqrt(own_tile / cells) * lax.rsqrt(outer_tile / cells + 1e-06))[0:1, :]
    clip = jnp.minimum(1.0, 0.5 * lax.rsqrt(total / (nb * cells) + 1e-06))[0:1, :]

    pairs = chunks_of(n)
    def home(a, j, to):
        return remote(
            cbuf.at[a, 0:plan.most[j]], fbuf.at[plan.base[j]:plan.base[j] + plan.most[j]],
            f_send.at[a], f_recv.at[j], to, col,
        )

    def step_of(at, a):
        lanes = pl.ds(pl.multiple_of(lax.rem(me + a, n) * width, width), width)
        direction = jnp.where(filled, clip * (graft * outer[at, lanes]), 0.0)
        following = 0.9 * mv[at, lanes].astype(F32) + direction
        nm[at, lanes] = following.astype(BF16)
        return (-0.8 * (0.9 * following + direction)).astype(BF16)

    def outward(q, pair):
        def part(i):
            at = pl.ds(pl.multiple_of(i * tile, tile), tile)
            for h, a in enumerate(pair):
                ubuf[q, at, h * width:(h + 1) * width] = step_of(at, a)

        loop(0, rows // tile, part)
        rbufs[q][col] = ubuf[q, pl.ds(col * slab, slab), 0:len(pair) * width]

        def back(a):
            to = lax.rem(col + a, g)
            remote(
                ubuf.at[q, pl.ds(to * slab, slab), 0:len(pair) * width], rbufs[q].at[col],
                u_send.at[q], u_recv.at[q], me, to,
            ).start()

        loop(1, g, back)

    def homeward(q, pair):
        remote(
            rbufs[q].at[0:g - 1], rbufs[q].at[0:g - 1], u_send.at[q], u_recv.at[q], me, col
        ).wait_recv()

        def gather(r):
            piece = rbufs[q][tab[plan.slot + r]]
            for h, a in enumerate(pair):
                cbuf[a, r] = piece[:, h * width:(h + 1) * width]

        loop(0, g, gather)
        for j in range(1, n):
            @pl.when(me == j)
            def _():
                for a in pair:
                    if a == 0:
                        fbuf[plan.base[j]:plan.base[j] + plan.most[j]] = (
                            cbuf[a, 0:plan.most[j]]
                        )
                    else:
                        home(a, j, lax.rem(me + a, n)).start()

    store = pltpu.make_async_copy(nm, new_momentum.at[0], load_sem.at[5])

    def across(a):
        return remote(direct.at[a], zland, h_send.at[a], h_recv, lax.rem(me + a, n), col)

    def scatter():
        fbuf[col] = zland[pl.ds(col * slab, slab), :]

        def drop(a):
            to = lax.rem(col + a, g)
            remote(
                zland.at[pl.ds(to * slab, slab), :], fbuf.at[col], g_send, g_recv, me, to
            ).start()

        loop(1, g, drop)

    @pl.when(me == 0)
    def _():
        for a in (a for pair in pairs for a in pair):
            def part(i):
                at = pl.ds(pl.multiple_of(i * tile, tile), tile)
                if a == 0:
                    zland[at, :] = step_of(at, a)
                else:
                    direct[a, at, :] = step_of(at, a)

            loop(0, rows // tile, part)
            if a != 0:
                across(a).start()
        store.start()
        scatter()

    @pl.when(me != 0)
    def _():
        for q, pair in enumerate(pairs):
            outward(q, pair)
            if q > 0:
                homeward(q - 1, pairs[q - 1])
        store.start()
        across(0).wait_recv()
        scatter()
        homeward(len(pairs) - 1, pairs[-1])

    for j in range(1, n):
        @pl.when(me != j)
        def _():
            home(0, j, me).wait_recv()

    scattered = remote(fbuf.at[0:g - 1], fbuf.at[0:g - 1], g_send, g_recv, me, col)
    scattered.wait_recv()

    keep = pltpu.make_async_copy(fbuf, pieces, load_sem.at[0])
    keep.start()
    store.wait()
    keep.wait()
    for way in ways:
        remote(way[2], way[1], ring_send.at[way[3]], ring_recv.at[0, 0], me, col).wait_send()

    @pl.when(me != 0)
    def _():
        for line in lines:
            remote(
                line[1].at[LAG:g], line[1].at[LAG:g], z_send.at[line[2]], line[3].at[0], me, col
            ).wait_send()

    remote(abuf.at[1:g], abuf.at[1:g], a_send, a_recv, me, col).wait_send()
    remote(sqz.at[0:n - 1], sqz.at[0:n - 1], q_send.at[0], q_recv.at[0], me, col).wait_send()
    remote(sqs.at[0:g - 1], sqs.at[0:g - 1], q_send.at[1], q_recv.at[1], me, col).wait_send()
    scattered.wait_send()

    @pl.when(me == 0)
    def _():
        for a in range(1, n):
            across(a).wait_send()

    @pl.when(me != 0)
    def _():
        for q in range(len(pairs)):
            remote(
                rbufs[q].at[0:g - 1], rbufs[q].at[0:g - 1], u_send.at[q], u_recv.at[q], me, col
            ).wait_send()

    for j in range(1, n):
        @pl.when(me == j)
        def _():
            for a in range(1, n):
                home(a, j, me).wait_send()


def last_kernel(plan, pieces, following, tab, update, new_momentum, through, held, placed, sems):
    step = plan.rows // 4
    rows = [slice(i * step, (i + 1) * step) for i in range(4)]
    fetch = pltpu.make_async_copy(pieces, held, sems.at[8])
    reads = [
        pltpu.make_async_copy(following.at[0, r], through.at[r], sems.at[i])
        for i, r in enumerate(rows)
    ]
    writes = [
        pltpu.make_async_copy(through.at[r], new_momentum.at[0, r], sems.at[4 + i])
        for i, r in enumerate(rows)
    ]
    fetch.start()
    for read in reads:
        read.start()
    fetch.wait()

    def place(b, c):
        placed[b] = held[tab[plan.where + b]]
        return c

    lax.fori_loop(0, plan.blocks, place, 0)
    put = pltpu.make_async_copy(placed, update, sems.at[9])
    put.start()
    for read, write in zip(reads, writes):
        read.wait()
        write.start()
    for write in writes:
        write.wait()
    put.wait()


def per_device(planes, groups, grads, left, right, momentum, block_order, owner_counts):
    blocks, slab, cols = grads.shape[1:]
    rows = left.shape[1]
    plan = Plan(planes, groups, blocks, rows, cols)
    half, width = slab // 2, cols // planes
    smem = pl.BlockSpec(memory_space=pltpu.SMEM)
    table = pl.pallas_call(
        functools.partial(table_kernel, plan),
        out_shape=jax.ShapeDtypeStruct((plan.size,), jnp.int32),
        in_specs=[smem, smem],
        out_specs=smem,
        scratch_shapes=[pltpu.SMEM((64,), jnp.int32)],
    )(block_order, owner_counts)
    anywhere = pl.BlockSpec(memory_space=pl.ANY)
    dma = pltpu.SemaphoreType.DMA
    held = plan.blocks + plan.sends
    chunks = chunks_of(planes)
    pieces, following = pl.pallas_call(
        functools.partial(step_kernel, plan),
        out_shape=(
            jax.ShapeDtypeStruct((plan.slots, slab, width), BF16),
            jax.ShapeDtypeStruct((1, rows, cols), BF16),
        ),
        in_specs=[anywhere] * 4 + [smem],
        out_specs=(anywhere, anywhere),
        scratch_shapes=(
            [pltpu.VMEM((held, half, cols), BF16)] * 2
            + [pltpu.VMEM((plan.sends, half, cols), BF16)] * 4
            + [pltpu.VMEM((groups, half, cols), BF16)] * 2
            + [pltpu.VMEM((groups, slab, cols), BF16), pltpu.VMEM((rows, cols), BF16)]
            + [
                pltpu.VMEM((rows, rows), BF16),
                pltpu.VMEM((cols, cols), BF16),
                pltpu.VMEM((rows, cols), BF16),
                pltpu.VMEM((rows, cols), BF16),
                pltpu.VMEM((rows, cols), F32),
                pltpu.VMEM((rows, cols), BF16),
                pltpu.VMEM((len(chunks), rows, 2 * width), BF16),
                pltpu.VMEM((planes, groups, slab, width), BF16),
                pltpu.VMEM((plan.slots, slab, width), BF16),
                pltpu.VMEM((8, 128), F32),
                pltpu.VMEM((8, 128), F32),
                pltpu.VMEM((planes, 8, 128), F32),
                pltpu.VMEM((groups, 8, 128), F32),
            ]
            + [
                dma((6,)),
                dma((2,)),
                dma((2 * PARTS, plan.sends)),
                dma((2,)),
                dma((groups,)),
                dma((groups,)),
                dma,
                dma,
                dma((2,)),
                dma((2,)),
                dma((len(chunks),)),
                dma((len(chunks),)),
                dma((planes,)),
                dma((planes,)),
                pltpu.VMEM((planes, rows, width), BF16),
                pltpu.VMEM((rows, width), BF16),
                dma((planes,)),
                dma,
                dma,
                dma,
            ]
            + [pltpu.VMEM((groups, slab, len(c) * width), BF16) for c in chunks]
        ),
        compiler_params=pltpu.CompilerParams(
            collective_id=0, has_side_effects=True, vmem_limit_bytes=56 * 1024 * 1024
        ),
        cost_estimate=pl.CostEstimate(
            flops=2 * rows * cols * (rows + cols), bytes_accessed=2 * 13 * rows * cols // 2,
            transcendentals=0,
        ),
    )(grads, left, right, momentum, table)
    return pl.pallas_call(
        functools.partial(last_kernel, plan),
        out_shape=(
            jax.ShapeDtypeStruct((blocks, slab, width), BF16),
            jax.ShapeDtypeStruct((1, rows, cols), BF16),
        ),
        in_specs=[anywhere, anywhere, smem],
        out_specs=(anywhere, anywhere),
        scratch_shapes=[
            pltpu.VMEM((rows, cols), BF16),
            pltpu.VMEM((plan.slots, slab, width), BF16),
            pltpu.VMEM((blocks, slab, width), BF16),
            dma((10,)),
        ],
    )(pieces, following, table)


def solution(mesh):
    slots = P(("dp", "shard"), None, None)
    return jax.shard_map(
        functools.partial(per_device, mesh.shape["dp"], mesh.shape["shard"]),
        mesh=mesh,
        in_specs=(P("dp", None, "shard", None), slots, slots, slots, P(), P()),
        out_specs=(P(None, "shard", "dp"), slots),
        check_vma=False,
    )
```

```python
import functools

import jax
import jax.numpy as jnp
from jax import lax
from jax.experimental import pallas as pl
from jax.experimental.pallas import tpu as pltpu
from jax.sharding import PartitionSpec as P

MESH = pl.DeviceIdType.MESH
LAG = 3
PARTS = 1
SKEW = 3
EARLY = 18
F32 = jnp.float32
BF16 = jnp.bfloat16


class Plan:
    def __init__(self, planes, groups, blocks, rows, cols):
        self.planes, self.groups, self.blocks = planes, groups, blocks
        self.rows, self.cols = rows, cols
        extras = blocks - groups
        self.most = [groups] + [
            min(groups, (extras - (planes - 1 - j)) // j) for j in range(1, planes)
        ]
        self.base = [sum(self.most[:j]) for j in range(planes)]
        self.slots = sum(self.most)
        self.sends = max(extras - (planes - 2), LAG) + (planes - 2) * LAG
        place = 0
        for name, size in (
            ("before", self.sends),
            ("order", 2 * (self.sends + LAG)),
            ("first", groups),
            ("rank", groups),
            ("slot", groups),
            ("where", blocks),
            ("scalars", 16),
        ):
            setattr(self, name, place)
            place += size
        self.size = place


def chunks_of(n):
    return [(n // 2,)] + [(n // 2 - i, n // 2 + i) for i in range(1, n // 2)] + [(0,)]


def plane_order(n):
    low, high = list(range(n // 2, 0, -1)), list(range(n // 2 + 1, n))
    order = []
    while high:
        order += [high.pop(0), low.pop(0)]
    return order + low + [0]


def table_kernel(plan, order_ref, counts_ref, tab, held):
    n, g = plan.planes, plan.groups
    me, col = lax.axis_index("dp"), lax.axis_index("shard")
    prev, nxt = lax.rem(me + n - 1, n), lax.rem(me + 1, n)
    hist, start, rank, width = 0, 16, 32, 48
    for i in range(plan.first):
        tab[i] = 0
    for i in range(16):
        held[hist + i] = 0
        held[rank + i] = 0

    def tally(o, seen):
        p, mine = seen
        k = counts_ref[o]
        held[hist + k] = held[hist + k] + 1
        b = order_ref[p]
        tab[plan.first + o] = b
        tab[plan.where + b] = o
        tab[plan.rank + o] = jnp.where(k > me, mine, -1)
        tab[plan.slot + o] = 0
        tab[plan.slot + mine] = o
        return p + k, mine + jnp.where(k > me, 1, 0)

    lax.fori_loop(0, g, tally, (jnp.int32(0), jnp.int32(0)))
    run = jnp.int32(0)
    at = jnp.int32(0)
    for j in range(n - 1, -1, -1):
        run = run + held[hist + j + 1]
        wide = jnp.int32(LAG) if j == 0 else jnp.maximum(run, LAG)
        held[start + j] = at
        held[width + j] = wide
        at = at + wide
    total = at
    for r in range(LAG):
        b = tab[plan.first + lax.rem(col + r, g)]
        tab[plan.order + held[start] + r] = b
        tab[plan.order + held[start] + r + total] = b

    def group(o, p):
        count = counts_ref[o]

        def one(j, c):
            b = order_ref[p + j]
            r = held[rank + j]
            held[rank + j] = r + 1
            u = plan.order + held[start + j] + r
            tab[u] = b
            tab[u + total] = b
            offset = jnp.int32(plan.base[1])
            for i in range(2, n):
                offset = jnp.where(j >= i, plan.base[i], offset)
            tab[plan.where + b] = offset + r
            return c

        lax.fori_loop(1, count, one, 0)
        return p + count

    lax.fori_loop(0, g, group, jnp.int32(0))
    s = plan.scalars
    before, after, own = held[width + prev], held[width + nxt], held[width + me]
    tab[s + 0] = plan.order + held[start + prev]
    tab[s + 1] = before
    tab[s + 2] = total - before - own
    tab[s + 3] = plan.order + held[start + nxt] + after - 1 + total
    tab[s + 4] = after
    tab[s + 5] = total - after - 1
    tab[s + 6] = jnp.where(counts_ref[col] > me, 1, 0)


def step_kernel(
    plan,
    grads, left, right, momentum, tab,
    pieces, new_momentum,
    gp, gm, landp, landm, outp, outm, zp, zm, abuf, gblk,
    lv, rv, mv, inner, outer, nm, ubuf, cbuf, fbuf,
    sq_own, sq_mid, sqz, sqs, sq_sum,
    load_sem, ring_send, ring_recv, z_send, zp_recv, zm_recv, a_send, a_recv,
    q_send, q_recv, u_send, u_recv, f_send, f_recv,
    direct, zland, h_send, h_recv, g_send, g_recv,
    *rbufs,
):
    n, g, nb = plan.planes, plan.groups, plan.blocks
    rows, cols = plan.rows, plan.cols
    slab = rows // g
    half = slab // 2
    width = cols // n
    me, col = lax.axis_index("dp"), lax.axis_index("shard")
    ahead, behind = lax.rem(me + 1, n), lax.rem(me + n - 1, n)

    def loop(low, high, body):
        lax.fori_loop(low, high, lambda i, c: (body(i), c)[1], 0)

    def remote(src, dst, send, recv, dp, shard):
        return pltpu.make_async_remote_copy(
            src_ref=src, dst_ref=dst, send_sem=send, recv_sem=recv,
            device_id={"dp": dp, "shard": shard}, device_id_type=MESH,
        )

    load_p = pltpu.make_async_copy(grads.at[0, :, 0:half, :], gp.at[0:nb], load_sem.at[0])
    load_m = pltpu.make_async_copy(grads.at[0, :, half:slab, :], gm.at[0:nb], load_sem.at[1])
    load_p.start()
    load_m.start()
    loads = [
        pltpu.make_async_copy(src.at[0], dst, load_sem.at[2 + i])
        for i, (src, dst) in enumerate(((left, lv), (right, rv), (momentum, mv)))
    ]

    barrier = pltpu.get_barrier_semaphore()
    for a in range(1, n):
        pl.semaphore_signal(
            barrier, inc=1, device_id={"dp": lax.rem(me + a, n), "shard": col}, device_id_type=MESH
        )

    def greet(a):
        pl.semaphore_signal(
            barrier, inc=1, device_id={"dp": me, "shard": lax.rem(col + a, g)}, device_id_type=MESH
        )

    loop(1, g, greet)
    pl.semaphore_wait(barrier, n - 1 + g - 1)
    load_p.wait()
    load_m.wait()
    for load in loads:
        load.start()

    sc = plan.scalars
    ways = (
        (gp, landp, outp, 0, ahead, tab[sc], 1, tab[sc + 1]),
        (gm, landm, outm, 1, behind, tab[sc + 3], -1, tab[sc + 4]),
    )
    parts = tuple(slice(h * (cols // PARTS), (h + 1) * (cols // PARTS)) for h in range(PARTS))

    def passing(way, k, h):
        _, land, out, d, to, _, _, _ = way
        return remote(
            out.at[k, :, parts[h]], land.at[k, :, parts[h]],
            ring_send.at[d], ring_recv.at[PARTS * d + h, k], to, col,
        )

    def take(k, h):
        for way in ways:
            held, land, _, _, _, start, sign, lag = way
            passing(way, k, h).wait_recv()
            own = held[tab[jnp.maximum(start + sign * (lag + k), 0)], :, parts[h]]
            held[nb + k, :, parts[h]] = land[k, :, parts[h]] + own

    def give(k, h):
        for way in ways:
            held, _, out, _, _, start, sign, lag = way
            source = jnp.where(k < lag, tab[jnp.maximum(start + sign * k, 0)], nb + k - lag)
            out[k, :, parts[h]] = held[source, :, parts[h]]
            passing(way, k, h).start()

    def ring(k, taking=True, giving=True):
        for h in range(PARTS):
            if taking:
                take(k - LAG, h)
            if giving:
                give(k, h)

    def exchange(t):
        @pl.when(t == 0)
        def _():
            gblk[pl.ds(col * slab, slab), :] = abuf[0]

        @pl.when(t > 0)
        def _():
            remote(
                abuf.at[t], gblk.at[pl.ds(col * slab, slab), :], a_send, a_recv,
                me, lax.rem(t + col, g),
            ).start()

    def count_squares(t, counted):
        x = abuf[t].astype(F32)
        sq_sum[...] += jnp.where(counted, jnp.sum(x * x, axis=0, keepdims=True), 0.0)

    far = SKEW * (n - 1)
    lines = (
        (gp, zp, 0, zp_recv, ahead, me - 1, 1),
        (gm, zm, 1, zm_recv, behind, n - 1 - me, n - 1),
    )
    begin, ready = max(plan.sends - EARLY, LAG), plan.sends + LAG
    end = max(begin + far + g - LAG, ready + g)

    def along(line, q):
        _, zbuf, d, recv, to, _, _ = line
        return remote(zbuf.at[q], zbuf.at[q], z_send.at[d], recv.at[q], to, col)

    def first_block(line, q):
        return line[0][tab[plan.first + lax.rem(q + col, g)]]

    def chain(t):
        @pl.when(me != 0)
        def _():
            for line in lines:
                zbuf, hops, source = line[1], line[5], line[6]
                q = t - begin - SKEW * hops + LAG

                @pl.when((q >= LAG) & (q < g))
                def _():
                    @pl.when(me == source)
                    def _():
                        zbuf[q] = first_block(line, q)

                    @pl.when(me != source)
                    def _():
                        along(line, q).wait_recv()
                        zbuf[q] = zbuf[q] + first_block(line, q)

                    along(line, q).start()

        @pl.when((me == 0) & (t >= begin + far) & (t < begin + far + g - LAG))
        def _():
            q = t - begin - far + LAG
            for line, low in zip(lines, (0, half)):
                along(line, q).wait_recv()
                abuf[q, low:low + half, :] = line[1][q] + first_block(line, q)
            exchange(q)
            count_squares(q, True)

    def settle(t):
        i = t - ready

        @pl.when((i < g) & ((me != 0) | (i < LAG)))
        def _():
            listed = tab[plan.rank + lax.rem(i + col, g)]
            r = jnp.where(me == 0, i, jnp.maximum(listed, 0))
            abuf[i, 0:half, :] = gp[nb + tab[sc + 2] + r]
            abuf[i, half:slab, :] = gm[nb + tab[sc + 5] - r]
            exchange(i)
            count_squares(i, listed >= 0)

    sq_sum[...] = jnp.zeros_like(sq_sum)
    loop(0, LAG, lambda k: ring(k, taking=False))
    loop(LAG, begin, ring)
    loop(begin, plan.sends, lambda k: (ring(k), chain(k)))
    loop(plan.sends, ready, lambda k: (ring(k, giving=False), chain(k)))
    loop(ready, end, lambda k: (chain(k), settle(k)))

    sq_own[...] = jnp.full((8, 128), jnp.sum(sq_sum[...]), F32)
    sqz[me] = sq_own[...]
    for a in range(1, n):
        to = lax.rem(me + a, n)
        remote(sq_own, sqz.at[me], q_send.at[0], q_recv.at[0], to, col).start()

    remote(
        gblk.at[0:(g - 1) * slab], gblk.at[0:(g - 1) * slab], a_send, a_recv, me, col
    ).wait_recv()
    filled = tab[sc + 6] > 0
    tile = min(128, rows)
    for load in loads:
        load.wait()
    strip = 256

    def first_product(i, acc):
        at = pl.ds(pl.multiple_of(i * strip, strip), strip)
        inner[:, at] = jnp.dot(lv[...], gblk[:, at], preferred_element_type=F32).astype(BF16)
        x = gblk[:, at].astype(F32)
        return acc + jnp.sum(x * x, axis=0, keepdims=True)

    grad_square = jnp.sum(
        lax.fori_loop(0, cols // strip, first_product, jnp.zeros((1, strip), F32))
    )
    own_tile = jnp.full((8, 128), grad_square, F32)
    remote(sqz.at[0:n - 1], sqz.at[0:n - 1], q_send.at[0], q_recv.at[0], me, col).wait_recv()
    mid = sqz[0]
    for j in range(1, n):
        mid = mid + sqz[j]
    sq_mid[...] = mid
    sqs[col] = mid

    def tell(a):
        remote(
            sq_mid, sqs.at[col], q_send.at[1], q_recv.at[1], me, lax.rem(col + a, g)
        ).start()

    loop(1, g, tell)

    def second_product(i, acc):
        at = pl.ds(pl.multiple_of(i * strip, strip), strip)
        x = jnp.dot(inner[...], rv[:, at], preferred_element_type=F32)
        outer[:, at] = x
        return acc + jnp.sum(x * x, axis=0, keepdims=True)

    outer_square = jnp.sum(
        lax.fori_loop(0, cols // strip, second_product, jnp.zeros((1, strip), F32))
    )
    remote(sqs.at[0:g - 1], sqs.at[0:g - 1], q_send.at[1], q_recv.at[1], me, col).wait_recv()
    total = lax.fori_loop(0, g, lambda j, acc: acc + sqs[j], jnp.zeros((8, 128), F32))
    cells = float(rows * cols)
    outer_tile = jnp.full((8, 128), outer_square, F32)
    graft = (jnp.sqrt(own_tile / cells) * lax.rsqrt(outer_tile / cells + 1e-06))[0:1, :]
    clip = jnp.minimum(1.0, 0.5 * lax.rsqrt(total / (nb * cells) + 1e-06))[0:1, :]

    pairs = chunks_of(n)
    def home(a, j, to):
        return remote(
            cbuf.at[a, 0:plan.most[j]], fbuf.at[plan.base[j]:plan.base[j] + plan.most[j]],
            f_send.at[a], f_recv.at[j], to, col,
        )

    def step_of(at, a):
        lanes = pl.ds(pl.multiple_of(lax.rem(me + a, n) * width, width), width)
        direction = jnp.where(filled, clip * (graft * outer[at, lanes]), 0.0)
        following = 0.9 * mv[at, lanes].astype(F32) + direction
        nm[at, lanes] = following.astype(BF16)
        return (-0.8 * (0.9 * following + direction)).astype(BF16)

    def outward(q, pair):
        def part(i):
            at = pl.ds(pl.multiple_of(i * tile, tile), tile)
            for h, a in enumerate(pair):
                ubuf[q, at, h * width:(h + 1) * width] = step_of(at, a)

        loop(0, rows // tile, part)
        rbufs[q][col] = ubuf[q, pl.ds(col * slab, slab), 0:len(pair) * width]

        def back(a):
            to = lax.rem(col + a, g)
            remote(
                ubuf.at[q, pl.ds(to * slab, slab), 0:len(pair) * width], rbufs[q].at[col],
                u_send.at[q], u_recv.at[q], me, to,
            ).start()

        loop(1, g, back)

    def homeward(q, pair):
        remote(
            rbufs[q].at[0:g - 1], rbufs[q].at[0:g - 1], u_send.at[q], u_recv.at[q], me, col
        ).wait_recv()

        def gather(r):
            piece = rbufs[q][tab[plan.slot + r]]
            for h, a in enumerate(pair):
                cbuf[a, r] = piece[:, h * width:(h + 1) * width]

        loop(0, g, gather)
        for j in range(1, n):
            @pl.when(me == j)
            def _():
                for a in pair:
                    if a == 0:
                        fbuf[plan.base[j]:plan.base[j] + plan.most[j]] = (
                            cbuf[a, 0:plan.most[j]]
                        )
                    else:
                        home(a, j, lax.rem(me + a, n)).start()

    store = pltpu.make_async_copy(nm, new_momentum.at[0], load_sem.at[5])

    def across(a):
        return remote(direct.at[a], zland, h_send.at[a], h_recv, lax.rem(me + a, n), col)

    def scatter():
        fbuf[col] = zland[pl.ds(col * slab, slab), :]

        def drop(a):
            to = lax.rem(col + a, g)
            remote(
                zland.at[pl.ds(to * slab, slab), :], fbuf.at[col], g_send, g_recv, me, to
            ).start()

        loop(1, g, drop)

    @pl.when(me == 0)
    def _():
        for a in plane_order(n):
            def part(i):
                at = pl.ds(pl.multiple_of(i * tile, tile), tile)
                if a == 0:
                    zland[at, :] = step_of(at, a)
                else:
                    direct[a, at, :] = step_of(at, a)

            loop(0, rows // tile, part)
            if a != 0:
                across(a).start()
        store.start()
        scatter()

    @pl.when(me != 0)
    def _():
        for q, pair in enumerate(pairs):
            outward(q, pair)
            if q > 0:
                homeward(q - 1, pairs[q - 1])
        store.start()
        across(0).wait_recv()
        scatter()
        homeward(len(pairs) - 1, pairs[-1])

    for j in range(1, n):
        @pl.when(me != j)
        def _():
            home(0, j, me).wait_recv()

    scattered = remote(fbuf.at[0:g - 1], fbuf.at[0:g - 1], g_send, g_recv, me, col)
    scattered.wait_recv()

    keep = pltpu.make_async_copy(fbuf, pieces, load_sem.at[0])
    keep.start()
    store.wait()
    keep.wait()
    for way in ways:
        remote(way[2], way[1], ring_send.at[way[3]], ring_recv.at[0, 0], me, col).wait_send()

    @pl.when(me != 0)
    def _():
        for line in lines:
            remote(
                line[1].at[LAG:g], line[1].at[LAG:g], z_send.at[line[2]], line[3].at[0], me, col
            ).wait_send()

    remote(abuf.at[1:g], abuf.at[1:g], a_send, a_recv, me, col).wait_send()
    remote(sqz.at[0:n - 1], sqz.at[0:n - 1], q_send.at[0], q_recv.at[0], me, col).wait_send()
    remote(sqs.at[0:g - 1], sqs.at[0:g - 1], q_send.at[1], q_recv.at[1], me, col).wait_send()
    scattered.wait_send()

    @pl.when(me == 0)
    def _():
        for a in range(1, n):
            across(a).wait_send()

    @pl.when(me != 0)
    def _():
        for q in range(len(pairs)):
            remote(
                rbufs[q].at[0:g - 1], rbufs[q].at[0:g - 1], u_send.at[q], u_recv.at[q], me, col
            ).wait_send()

    for j in range(1, n):
        @pl.when(me == j)
        def _():
            for a in range(1, n):
                home(a, j, me).wait_send()


def last_kernel(plan, pieces, following, tab, update, new_momentum, through, held, placed, sems):
    step = plan.rows // 4
    rows = [slice(i * step, (i + 1) * step) for i in range(4)]
    fetch = pltpu.make_async_copy(pieces, held, sems.at[8])
    reads = [
        pltpu.make_async_copy(following.at[0, r], through.at[r], sems.at[i])
        for i, r in enumerate(rows)
    ]
    writes = [
        pltpu.make_async_copy(through.at[r], new_momentum.at[0, r], sems.at[4 + i])
        for i, r in enumerate(rows)
    ]
    fetch.start()
    for read in reads:
        read.start()
    fetch.wait()

    def place(b, c):
        placed[b] = held[tab[plan.where + b]]
        return c

    lax.fori_loop(0, plan.blocks, place, 0)
    put = pltpu.make_async_copy(placed, update, sems.at[9])
    put.start()
    for read, write in zip(reads, writes):
        read.wait()
        write.start()
    for write in writes:
        write.wait()
    put.wait()


def per_device(planes, groups, grads, left, right, momentum, block_order, owner_counts):
    blocks, slab, cols = grads.shape[1:]
    rows = left.shape[1]
    plan = Plan(planes, groups, blocks, rows, cols)
    half, width = slab // 2, cols // planes
    smem = pl.BlockSpec(memory_space=pltpu.SMEM)
    table = pl.pallas_call(
        functools.partial(table_kernel, plan),
        out_shape=jax.ShapeDtypeStruct((plan.size,), jnp.int32),
        in_specs=[smem, smem],
        out_specs=smem,
        scratch_shapes=[pltpu.SMEM((64,), jnp.int32)],
    )(block_order, owner_counts)
    anywhere = pl.BlockSpec(memory_space=pl.ANY)
    dma = pltpu.SemaphoreType.DMA
    held = plan.blocks + plan.sends
    chunks = chunks_of(planes)
    pieces, following = pl.pallas_call(
        functools.partial(step_kernel, plan),
        out_shape=(
            jax.ShapeDtypeStruct((plan.slots, slab, width), BF16),
            jax.ShapeDtypeStruct((1, rows, cols), BF16),
        ),
        in_specs=[anywhere] * 4 + [smem],
        out_specs=(anywhere, anywhere),
        scratch_shapes=(
            [pltpu.VMEM((held, half, cols), BF16)] * 2
            + [pltpu.VMEM((plan.sends, half, cols), BF16)] * 4
            + [pltpu.VMEM((groups, half, cols), BF16)] * 2
            + [pltpu.VMEM((groups, slab, cols), BF16), pltpu.VMEM((rows, cols), BF16)]
            + [
                pltpu.VMEM((rows, rows), BF16),
                pltpu.VMEM((cols, cols), BF16),
                pltpu.VMEM((rows, cols), BF16),
                pltpu.VMEM((rows, cols), BF16),
                pltpu.VMEM((rows, cols), F32),
                pltpu.VMEM((rows, cols), BF16),
                pltpu.VMEM((len(chunks), rows, 2 * width), BF16),
                pltpu.VMEM((planes, groups, slab, width), BF16),
                pltpu.VMEM((plan.slots, slab, width), BF16),
                pltpu.VMEM((8, 128), F32),
                pltpu.VMEM((8, 128), F32),
                pltpu.VMEM((planes, 8, 128), F32),
                pltpu.VMEM((groups, 8, 128), F32),
                pltpu.VMEM((1, cols), F32),
            ]
            + [
                dma((6,)),
                dma((2,)),
                dma((2 * PARTS, plan.sends)),
                dma((2,)),
                dma((groups,)),
                dma((groups,)),
                dma,
                dma,
                dma((2,)),
                dma((2,)),
                dma((len(chunks),)),
                dma((len(chunks),)),
                dma((planes,)),
                dma((planes,)),
                pltpu.VMEM((planes, rows, width), BF16),
                pltpu.VMEM((rows, width), BF16),
                dma((planes,)),
                dma,
                dma,
                dma,
            ]
            + [pltpu.VMEM((groups, slab, len(c) * width), BF16) for c in chunks]
        ),
        compiler_params=pltpu.CompilerParams(
            collective_id=0, has_side_effects=True, vmem_limit_bytes=56 * 1024 * 1024
        ),
        cost_estimate=pl.CostEstimate(
            flops=2 * rows * cols * (rows + cols), bytes_accessed=2 * 13 * rows * cols // 2,
            transcendentals=0,
        ),
    )(grads, left, right, momentum, table)
    return pl.pallas_call(
        functools.partial(last_kernel, plan),
        out_shape=(
            jax.ShapeDtypeStruct((blocks, slab, width), BF16),
            jax.ShapeDtypeStruct((1, rows, cols), BF16),
        ),
        in_specs=[anywhere, anywhere, smem],
        out_specs=(anywhere, anywhere),
        scratch_shapes=[
            pltpu.VMEM((rows, cols), BF16),
            pltpu.VMEM((plan.slots, slab, width), BF16),
            pltpu.VMEM((blocks, slab, width), BF16),
            dma((10,)),
        ],
    )(pieces, following, table)


def solution(mesh):
    slots = P(("dp", "shard"), None, None)
    return jax.shard_map(
        functools.partial(per_device, mesh.shape["dp"], mesh.shape["shard"]),
        mesh=mesh,
        in_specs=(P("dp", None, "shard", None), slots, slots, slots, P(), P()),
        out_specs=(P(None, "shard", "dp"), slots),
        check_vma=False,
    )
```

```python
import functools

import jax
import jax.numpy as jnp
from jax import lax
from jax.experimental import pallas as pl
from jax.experimental.pallas import tpu as pltpu
from jax.sharding import PartitionSpec as P

MESH = pl.DeviceIdType.MESH
LAG = 3
PARTS = 1
SKEW = 2
EARLY = 10
F32 = jnp.float32
BF16 = jnp.bfloat16


class Plan:
    def __init__(self, planes, groups, blocks, rows, cols):
        self.planes, self.groups, self.blocks = planes, groups, blocks
        self.rows, self.cols = rows, cols
        extras = blocks - groups
        self.most = [groups] + [
            min(groups, (extras - (planes - 1 - j)) // j) for j in range(1, planes)
        ]
        self.base = [sum(self.most[:j]) for j in range(planes)]
        self.slots = sum(self.most)
        self.sends = max(extras - (planes - 2), LAG) + (planes - 2) * LAG
        place = 0
        for name, size in (
            ("before", self.sends),
            ("order", 2 * (self.sends + LAG)),
            ("first", groups),
            ("rank", groups),
            ("slot", groups),
            ("where", blocks),
            ("scalars", 16),
        ):
            setattr(self, name, place)
            place += size
        self.size = place


def chunks_of(n):
    return [(n // 2,)] + [(n // 2 - i, n // 2 + i) for i in range(1, n // 2)] + [(0,)]


def plane_order(n):
    low, high = list(range(n // 2, 0, -1)), list(range(n // 2 + 1, n))
    order = []
    while high:
        order += [high.pop(0), low.pop(0)]
    return order + low + [0]


def table_kernel(plan, order_ref, counts_ref, tab, held):
    n, g = plan.planes, plan.groups
    me, col = lax.axis_index("dp"), lax.axis_index("shard")
    prev, nxt = lax.rem(me + n - 1, n), lax.rem(me + 1, n)
    hist, start, rank, width = 0, 16, 32, 48
    for i in range(plan.first):
        tab[i] = 0
    for i in range(16):
        held[hist + i] = 0
        held[rank + i] = 0

    def tally(o, seen):
        p, mine = seen
        k = counts_ref[o]
        held[hist + k] = held[hist + k] + 1
        b = order_ref[p]
        tab[plan.first + o] = b
        tab[plan.where + b] = o
        tab[plan.rank + o] = jnp.where(k > me, mine, -1)
        tab[plan.slot + o] = 0
        tab[plan.slot + mine] = o
        return p + k, mine + jnp.where(k > me, 1, 0)

    lax.fori_loop(0, g, tally, (jnp.int32(0), jnp.int32(0)))
    run = jnp.int32(0)
    at = jnp.int32(0)
    for j in range(n - 1, -1, -1):
        run = run + held[hist + j + 1]
        wide = jnp.int32(LAG) if j == 0 else jnp.maximum(run, LAG)
        held[start + j] = at
        held[width + j] = wide
        at = at + wide
    total = at
    for r in range(LAG):
        b = tab[plan.first + lax.rem(col + r, g)]
        tab[plan.order + held[start] + r] = b
        tab[plan.order + held[start] + r + total] = b

    def group(o, p):
        count = counts_ref[o]

        def one(j, c):
            b = order_ref[p + j]
            r = held[rank + j]
            held[rank + j] = r + 1
            u = plan.order + held[start + j] + r
            tab[u] = b
            tab[u + total] = b
            offset = jnp.int32(plan.base[1])
            for i in range(2, n):
                offset = jnp.where(j >= i, plan.base[i], offset)
            tab[plan.where + b] = offset + r
            return c

        lax.fori_loop(1, count, one, 0)
        return p + count

    lax.fori_loop(0, g, group, jnp.int32(0))
    s = plan.scalars
    before, after, own = held[width + prev], held[width + nxt], held[width + me]
    tab[s + 0] = plan.order + held[start + prev]
    tab[s + 1] = before
    tab[s + 2] = total - before - own
    tab[s + 3] = plan.order + held[start + nxt] + after - 1 + total
    tab[s + 4] = after
    tab[s + 5] = total - after - 1
    tab[s + 6] = jnp.where(counts_ref[col] > me, 1, 0)


def step_kernel(
    plan,
    grads, left, right, momentum, tab,
    pieces, new_momentum,
    gp, gm, landp, landm, outp, outm, zp, zm, abuf, gblk,
    lv, rv, mv, inner, outer, nm, ubuf, cbuf, fbuf,
    sq_own, sq_mid, sqz, sqs, sq_sum,
    load_sem, ring_send, ring_recv, z_send, zp_recv, zm_recv, a_send, a_recv,
    q_send, q_recv, u_send, u_recv, f_send, f_recv,
    direct, zland, h_send, h_recv, g_send, g_recv,
    *rbufs,
):
    n, g, nb = plan.planes, plan.groups, plan.blocks
    rows, cols = plan.rows, plan.cols
    slab = rows // g
    half = slab // 2
    width = cols // n
    me, col = lax.axis_index("dp"), lax.axis_index("shard")
    ahead, behind = lax.rem(me + 1, n), lax.rem(me + n - 1, n)

    def loop(low, high, body):
        lax.fori_loop(low, high, lambda i, c: (body(i), c)[1], 0)

    def remote(src, dst, send, recv, dp, shard):
        return pltpu.make_async_remote_copy(
            src_ref=src, dst_ref=dst, send_sem=send, recv_sem=recv,
            device_id={"dp": dp, "shard": shard}, device_id_type=MESH,
        )

    load_p = pltpu.make_async_copy(grads.at[0, :, 0:half, :], gp.at[0:nb], load_sem.at[0])
    load_m = pltpu.make_async_copy(grads.at[0, :, half:slab, :], gm.at[0:nb], load_sem.at[1])
    load_p.start()
    load_m.start()
    loads = [
        pltpu.make_async_copy(src.at[0], dst, load_sem.at[2 + i])
        for i, (src, dst) in enumerate(((left, lv), (right, rv), (momentum, mv)))
    ]

    barrier = pltpu.get_barrier_semaphore()
    for a in range(1, n):
        pl.semaphore_signal(
            barrier, inc=1, device_id={"dp": lax.rem(me + a, n), "shard": col}, device_id_type=MESH
        )

    def greet(a):
        pl.semaphore_signal(
            barrier, inc=1, device_id={"dp": me, "shard": lax.rem(col + a, g)}, device_id_type=MESH
        )

    loop(1, g, greet)
    pl.semaphore_wait(barrier, n - 1 + g - 1)
    load_p.wait()
    load_m.wait()
    for load in loads:
        load.start()

    sc = plan.scalars
    ways = (
        (gp, landp, outp, 0, ahead, tab[sc], 1, tab[sc + 1]),
        (gm, landm, outm, 1, behind, tab[sc + 3], -1, tab[sc + 4]),
    )
    parts = tuple(slice(h * (cols // PARTS), (h + 1) * (cols // PARTS)) for h in range(PARTS))

    def passing(way, k, h):
        _, land, out, d, to, _, _, _ = way
        return remote(
            out.at[k, :, parts[h]], land.at[k, :, parts[h]],
            ring_send.at[d], ring_recv.at[PARTS * d + h, k], to, col,
        )

    def take(k, h):
        for way in ways:
            held, land, _, _, _, start, sign, lag = way
            passing(way, k, h).wait_recv()
            own = held[tab[jnp.maximum(start + sign * (lag + k), 0)], :, parts[h]]
            held[nb + k, :, parts[h]] = land[k, :, parts[h]] + own

    def give(k, h):
        for way in ways:
            held, _, out, _, _, start, sign, lag = way
            source = jnp.where(k < lag, tab[jnp.maximum(start + sign * k, 0)], nb + k - lag)
            out[k, :, parts[h]] = held[source, :, parts[h]]
            passing(way, k, h).start()

    def ring(k, taking=True, giving=True):
        for h in range(PARTS):
            if taking:
                take(k - LAG, h)
            if giving:
                give(k, h)

    def exchange(t):
        @pl.when(t == 0)
        def _():
            gblk[pl.ds(col * slab, slab), :] = abuf[0]

        @pl.when(t > 0)
        def _():
            remote(
                abuf.at[t], gblk.at[pl.ds(col * slab, slab), :], a_send, a_recv,
                me, lax.rem(t + col, g),
            ).start()

    def count_squares(t, counted):
        x = abuf[t].astype(F32)
        sq_sum[...] += jnp.where(counted, jnp.sum(x * x, axis=0, keepdims=True), 0.0)

    far = SKEW * (n - 1)
    lines = (
        (gp, zp, 0, zp_recv, ahead, me - 1, 1),
        (gm, zm, 1, zm_recv, behind, n - 1 - me, n - 1),
    )
    begin, ready = max(plan.sends - EARLY, LAG), plan.sends + LAG
    end = max(begin + far + g - LAG, ready + g)

    def along(line, q):
        _, zbuf, d, recv, to, _, _ = line
        return remote(zbuf.at[q], zbuf.at[q], z_send.at[d], recv.at[q], to, col)

    def first_block(line, q):
        return line[0][tab[plan.first + lax.rem(q + col, g)]]

    def chain(t):
        @pl.when(me != 0)
        def _():
            for line in lines:
                zbuf, hops, source = line[1], line[5], line[6]
                q = t - begin - SKEW * hops + LAG

                @pl.when((q >= LAG) & (q < g))
                def _():
                    @pl.when(me == source)
                    def _():
                        zbuf[q] = first_block(line, q)

                    @pl.when(me != source)
                    def _():
                        along(line, q).wait_recv()
                        zbuf[q] = zbuf[q] + first_block(line, q)

                    along(line, q).start()

        @pl.when((me == 0) & (t >= begin + far) & (t < begin + far + g - LAG))
        def _():
            q = t - begin - far + LAG
            for line, low in zip(lines, (0, half)):
                along(line, q).wait_recv()
                abuf[q, low:low + half, :] = line[1][q] + first_block(line, q)
            exchange(q)
            count_squares(q, True)

    def settle(t):
        i = t - ready

        @pl.when((i < g) & ((me != 0) | (i < LAG)))
        def _():
            listed = tab[plan.rank + lax.rem(i + col, g)]
            r = jnp.where(me == 0, i, jnp.maximum(listed, 0))
            abuf[i, 0:half, :] = gp[nb + tab[sc + 2] + r]
            abuf[i, half:slab, :] = gm[nb + tab[sc + 5] - r]
            exchange(i)
            count_squares(i, listed >= 0)

    sq_sum[...] = jnp.zeros_like(sq_sum)
    loop(0, LAG, lambda k: ring(k, taking=False))
    loop(LAG, begin, ring)
    loop(begin, plan.sends, lambda k: (ring(k), chain(k)))
    loop(plan.sends, ready, lambda k: (ring(k, giving=False), chain(k)))
    loop(ready, end, lambda k: (chain(k), settle(k)))

    sq_own[...] = jnp.full((8, 128), jnp.sum(sq_sum[...]), F32)
    sqz[me] = sq_own[...]
    for a in range(1, n):
        to = lax.rem(me + a, n)
        remote(sq_own, sqz.at[me], q_send.at[0], q_recv.at[0], to, col).start()

    remote(
        gblk.at[0:(g - 1) * slab], gblk.at[0:(g - 1) * slab], a_send, a_recv, me, col
    ).wait_recv()
    filled = tab[sc + 6] > 0
    tile = min(128, rows)
    for load in loads:
        load.wait()
    strip = 256

    def first_product(i, acc):
        at = pl.ds(pl.multiple_of(i * strip, strip), strip)
        inner[:, at] = jnp.dot(lv[...], gblk[:, at], preferred_element_type=F32).astype(BF16)
        x = gblk[:, at].astype(F32)
        return acc + jnp.sum(x * x, axis=0, keepdims=True)

    grad_square = jnp.sum(
        lax.fori_loop(0, cols // strip, first_product, jnp.zeros((1, strip), F32))
    )
    own_tile = jnp.full((8, 128), grad_square, F32)
    remote(sqz.at[0:n - 1], sqz.at[0:n - 1], q_send.at[0], q_recv.at[0], me, col).wait_recv()
    mid = sqz[0]
    for j in range(1, n):
        mid = mid + sqz[j]
    sq_mid[...] = mid
    sqs[col] = mid

    def tell(a):
        remote(
            sq_mid, sqs.at[col], q_send.at[1], q_recv.at[1], me, lax.rem(col + a, g)
        ).start()

    loop(1, g, tell)

    def second_product(i, acc):
        at = pl.ds(pl.multiple_of(i * strip, strip), strip)
        x = jnp.dot(inner[...], rv[:, at], preferred_element_type=F32)
        outer[:, at] = x
        return acc + jnp.sum(x * x, axis=0, keepdims=True)

    outer_square = jnp.sum(
        lax.fori_loop(0, cols // strip, second_product, jnp.zeros((1, strip), F32))
    )
    remote(sqs.at[0:g - 1], sqs.at[0:g - 1], q_send.at[1], q_recv.at[1], me, col).wait_recv()
    total = lax.fori_loop(0, g, lambda j, acc: acc + sqs[j], jnp.zeros((8, 128), F32))
    cells = float(rows * cols)
    outer_tile = jnp.full((8, 128), outer_square, F32)
    graft = (jnp.sqrt(own_tile / cells) * lax.rsqrt(outer_tile / cells + 1e-06))[0:1, :]
    clip = jnp.minimum(1.0, 0.5 * lax.rsqrt(total / (nb * cells) + 1e-06))[0:1, :]

    pairs = chunks_of(n)
    def home(a, j, to):
        return remote(
            cbuf.at[a, 0:plan.most[j]], fbuf.at[plan.base[j]:plan.base[j] + plan.most[j]],
            f_send.at[a], f_recv.at[j], to, col,
        )

    def step_of(at, a):
        lanes = pl.ds(pl.multiple_of(lax.rem(me + a, n) * width, width), width)
        direction = jnp.where(filled, clip * (graft * outer[at, lanes]), 0.0)
        following = 0.9 * mv[at, lanes].astype(F32) + direction
        nm[at, lanes] = following.astype(BF16)
        return (-0.8 * (0.9 * following + direction)).astype(BF16)

    def outward(q, pair):
        def part(i):
            at = pl.ds(pl.multiple_of(i * tile, tile), tile)
            for h, a in enumerate(pair):
                ubuf[q, at, h * width:(h + 1) * width] = step_of(at, a)

        loop(0, rows // tile, part)
        rbufs[q][col] = ubuf[q, pl.ds(col * slab, slab), 0:len(pair) * width]

        def back(a):
            to = lax.rem(col + a, g)
            remote(
                ubuf.at[q, pl.ds(to * slab, slab), 0:len(pair) * width], rbufs[q].at[col],
                u_send.at[q], u_recv.at[q], me, to,
            ).start()

        loop(1, g, back)

    def homeward(q, pair):
        remote(
            rbufs[q].at[0:g - 1], rbufs[q].at[0:g - 1], u_send.at[q], u_recv.at[q], me, col
        ).wait_recv()

        def gather(r):
            piece = rbufs[q][tab[plan.slot + r]]
            for h, a in enumerate(pair):
                cbuf[a, r] = piece[:, h * width:(h + 1) * width]

        loop(0, g, gather)
        for j in range(1, n):
            @pl.when(me == j)
            def _():
                for a in pair:
                    if a == 0:
                        fbuf[plan.base[j]:plan.base[j] + plan.most[j]] = (
                            cbuf[a, 0:plan.most[j]]
                        )
                    else:
                        home(a, j, lax.rem(me + a, n)).start()

    store = pltpu.make_async_copy(nm, new_momentum.at[0], load_sem.at[5])

    def across(a):
        return remote(direct.at[a], zland, h_send.at[a], h_recv, lax.rem(me + a, n), col)

    def scatter():
        fbuf[col] = zland[pl.ds(col * slab, slab), :]

        def drop(a):
            to = lax.rem(col + a, g)
            remote(
                zland.at[pl.ds(to * slab, slab), :], fbuf.at[col], g_send, g_recv, me, to
            ).start()

        loop(1, g, drop)

    @pl.when(me == 0)
    def _():
        for a in plane_order(n):
            def part(i):
                at = pl.ds(pl.multiple_of(i * tile, tile), tile)
                if a == 0:
                    zland[at, :] = step_of(at, a)
                else:
                    direct[a, at, :] = step_of(at, a)

            loop(0, rows // tile, part)
            if a != 0:
                across(a).start()
        store.start()
        scatter()

    @pl.when(me != 0)
    def _():
        for q, pair in enumerate(pairs):
            outward(q, pair)
            if q > 0:
                homeward(q - 1, pairs[q - 1])
        store.start()
        across(0).wait_recv()
        scatter()
        homeward(len(pairs) - 1, pairs[-1])

    for j in range(1, n):
        @pl.when(me != j)
        def _():
            home(0, j, me).wait_recv()

    scattered = remote(fbuf.at[0:g - 1], fbuf.at[0:g - 1], g_send, g_recv, me, col)
    scattered.wait_recv()

    keep = pltpu.make_async_copy(fbuf, pieces, load_sem.at[0])
    keep.start()
    store.wait()
    keep.wait()
    for way in ways:
        remote(way[2], way[1], ring_send.at[way[3]], ring_recv.at[0, 0], me, col).wait_send()

    @pl.when(me != 0)
    def _():
        for line in lines:
            remote(
                line[1].at[LAG:g], line[1].at[LAG:g], z_send.at[line[2]], line[3].at[0], me, col
            ).wait_send()

    remote(abuf.at[1:g], abuf.at[1:g], a_send, a_recv, me, col).wait_send()
    remote(sqz.at[0:n - 1], sqz.at[0:n - 1], q_send.at[0], q_recv.at[0], me, col).wait_send()
    remote(sqs.at[0:g - 1], sqs.at[0:g - 1], q_send.at[1], q_recv.at[1], me, col).wait_send()
    scattered.wait_send()

    @pl.when(me == 0)
    def _():
        for a in range(1, n):
            across(a).wait_send()

    @pl.when(me != 0)
    def _():
        for q in range(len(pairs)):
            remote(
                rbufs[q].at[0:g - 1], rbufs[q].at[0:g - 1], u_send.at[q], u_recv.at[q], me, col
            ).wait_send()

    for j in range(1, n):
        @pl.when(me == j)
        def _():
            for a in range(1, n):
                home(a, j, me).wait_send()


def last_kernel(plan, pieces, following, tab, update, new_momentum, through, held, placed, sems):
    step = plan.rows // 4
    rows = [slice(i * step, (i + 1) * step) for i in range(4)]
    fetch = pltpu.make_async_copy(pieces, held, sems.at[8])
    reads = [
        pltpu.make_async_copy(following.at[0, r], through.at[r], sems.at[i])
        for i, r in enumerate(rows)
    ]
    writes = [
        pltpu.make_async_copy(through.at[r], new_momentum.at[0, r], sems.at[4 + i])
        for i, r in enumerate(rows)
    ]
    fetch.start()
    for read in reads:
        read.start()
    fetch.wait()

    def place(b, c):
        placed[b] = held[tab[plan.where + b]]
        return c

    lax.fori_loop(0, plan.blocks, place, 0)
    put = pltpu.make_async_copy(placed, update, sems.at[9])
    put.start()
    for read, write in zip(reads, writes):
        read.wait()
        write.start()
    for write in writes:
        write.wait()
    put.wait()


def per_device(planes, groups, grads, left, right, momentum, block_order, owner_counts):
    blocks, slab, cols = grads.shape[1:]
    rows = left.shape[1]
    plan = Plan(planes, groups, blocks, rows, cols)
    half, width = slab // 2, cols // planes
    smem = pl.BlockSpec(memory_space=pltpu.SMEM)
    table = pl.pallas_call(
        functools.partial(table_kernel, plan),
        out_shape=jax.ShapeDtypeStruct((plan.size,), jnp.int32),
        in_specs=[smem, smem],
        out_specs=smem,
        scratch_shapes=[pltpu.SMEM((64,), jnp.int32)],
    )(block_order, owner_counts)
    anywhere = pl.BlockSpec(memory_space=pl.ANY)
    dma = pltpu.SemaphoreType.DMA
    held = plan.blocks + plan.sends
    chunks = chunks_of(planes)
    pieces, following = pl.pallas_call(
        functools.partial(step_kernel, plan),
        out_shape=(
            jax.ShapeDtypeStruct((plan.slots, slab, width), BF16),
            jax.ShapeDtypeStruct((1, rows, cols), BF16),
        ),
        in_specs=[anywhere] * 4 + [smem],
        out_specs=(anywhere, anywhere),
        scratch_shapes=(
            [pltpu.VMEM((held, half, cols), BF16)] * 2
            + [pltpu.VMEM((plan.sends, half, cols), BF16)] * 4
            + [pltpu.VMEM((groups, half, cols), BF16)] * 2
            + [pltpu.VMEM((groups, slab, cols), BF16), pltpu.VMEM((rows, cols), BF16)]
            + [
                pltpu.VMEM((rows, rows), BF16),
                pltpu.VMEM((cols, cols), BF16),
                pltpu.VMEM((rows, cols), BF16),
                pltpu.VMEM((rows, cols), BF16),
                pltpu.VMEM((rows, cols), F32),
                pltpu.VMEM((rows, cols), BF16),
                pltpu.VMEM((len(chunks), rows, 2 * width), BF16),
                pltpu.VMEM((planes, groups, slab, width), BF16),
                pltpu.VMEM((plan.slots, slab, width), BF16),
                pltpu.VMEM((8, 128), F32),
                pltpu.VMEM((8, 128), F32),
                pltpu.VMEM((planes, 8, 128), F32),
                pltpu.VMEM((groups, 8, 128), F32),
                pltpu.VMEM((1, cols), F32),
            ]
            + [
                dma((6,)),
                dma((2,)),
                dma((2 * PARTS, plan.sends)),
                dma((2,)),
                dma((groups,)),
                dma((groups,)),
                dma,
                dma,
                dma((2,)),
                dma((2,)),
                dma((len(chunks),)),
                dma((len(chunks),)),
                dma((planes,)),
                dma((planes,)),
                pltpu.VMEM((planes, rows, width), BF16),
                pltpu.VMEM((rows, width), BF16),
                dma((planes,)),
                dma,
                dma,
                dma,
            ]
            + [pltpu.VMEM((groups, slab, len(c) * width), BF16) for c in chunks]
        ),
        compiler_params=pltpu.CompilerParams(
            collective_id=0, has_side_effects=True, vmem_limit_bytes=56 * 1024 * 1024
        ),
        cost_estimate=pl.CostEstimate(
            flops=2 * rows * cols * (rows + cols), bytes_accessed=2 * 13 * rows * cols // 2,
            transcendentals=0,
        ),
    )(grads, left, right, momentum, table)
    return pl.pallas_call(
        functools.partial(last_kernel, plan),
        out_shape=(
            jax.ShapeDtypeStruct((blocks, slab, width), BF16),
            jax.ShapeDtypeStruct((1, rows, cols), BF16),
        ),
        in_specs=[anywhere, anywhere, smem],
        out_specs=(anywhere, anywhere),
        scratch_shapes=[
            pltpu.VMEM((rows, cols), BF16),
            pltpu.VMEM((plan.slots, slab, width), BF16),
            pltpu.VMEM((blocks, slab, width), BF16),
            dma((10,)),
        ],
    )(pieces, following, table)


def solution(mesh):
    slots = P(("dp", "shard"), None, None)
    return jax.shard_map(
        functools.partial(per_device, mesh.shape["dp"], mesh.shape["shard"]),
        mesh=mesh,
        in_specs=(P("dp", None, "shard", None), slots, slots, slots, P(), P()),
        out_specs=(P(None, "shard", "dp"), slots),
        check_vma=False,
    )
```

```python
import functools

import jax
import jax.numpy as jnp
from jax import lax
from jax.experimental import pallas as pl
from jax.experimental.pallas import tpu as pltpu
from jax.sharding import PartitionSpec as P

MESH = pl.DeviceIdType.MESH
LAG = 3
PARTS = 1
SKEW = 4
EARLY = 24
F32 = jnp.float32
BF16 = jnp.bfloat16


class Plan:
    def __init__(self, planes, groups, blocks, rows, cols):
        self.planes, self.groups, self.blocks = planes, groups, blocks
        self.rows, self.cols = rows, cols
        extras = blocks - groups
        self.most = [groups] + [
            min(groups, (extras - (planes - 1 - j)) // j) for j in range(1, planes)
        ]
        self.base = [sum(self.most[:j]) for j in range(planes)]
        self.slots = sum(self.most)
        self.sends = max(extras - (planes - 2), LAG) + (planes - 2) * LAG
        place = 0
        for name, size in (
            ("before", self.sends),
            ("order", 2 * (self.sends + LAG)),
            ("first", groups),
            ("rank", groups),
            ("slot", groups),
            ("where", blocks),
            ("scalars", 16),
        ):
            setattr(self, name, place)
            place += size
        self.size = place


def chunks_of(n):
    return [(n // 2,)] + [(n // 2 - i, n // 2 + i) for i in range(1, n // 2)] + [(0,)]


def plane_order(n):
    low, high = list(range(n // 2, 0, -1)), list(range(n // 2 + 1, n))
    order = []
    while high:
        order += [high.pop(0), low.pop(0)]
    return order + low + [0]


def table_kernel(plan, order_ref, counts_ref, tab, held):
    n, g = plan.planes, plan.groups
    me, col = lax.axis_index("dp"), lax.axis_index("shard")
    prev, nxt = lax.rem(me + n - 1, n), lax.rem(me + 1, n)
    hist, start, rank, width = 0, 16, 32, 48
    for i in range(plan.first):
        tab[i] = 0
    for i in range(16):
        held[hist + i] = 0
        held[rank + i] = 0

    def tally(o, seen):
        p, mine = seen
        k = counts_ref[o]
        held[hist + k] = held[hist + k] + 1
        b = order_ref[p]
        tab[plan.first + o] = b
        tab[plan.where + b] = o
        tab[plan.rank + o] = jnp.where(k > me, mine, -1)
        tab[plan.slot + o] = 0
        tab[plan.slot + mine] = o
        return p + k, mine + jnp.where(k > me, 1, 0)

    lax.fori_loop(0, g, tally, (jnp.int32(0), jnp.int32(0)))
    run = jnp.int32(0)
    at = jnp.int32(0)
    for j in range(n - 1, -1, -1):
        run = run + held[hist + j + 1]
        wide = jnp.int32(LAG) if j == 0 else jnp.maximum(run, LAG)
        held[start + j] = at
        held[width + j] = wide
        at = at + wide
    total = at
    for r in range(LAG):
        b = tab[plan.first + lax.rem(col + r, g)]
        tab[plan.order + held[start] + r] = b
        tab[plan.order + held[start] + r + total] = b

    def group(o, p):
        count = counts_ref[o]

        def one(j, c):
            b = order_ref[p + j]
            r = held[rank + j]
            held[rank + j] = r + 1
            u = plan.order + held[start + j] + r
            tab[u] = b
            tab[u + total] = b
            offset = jnp.int32(plan.base[1])
            for i in range(2, n):
                offset = jnp.where(j >= i, plan.base[i], offset)
            tab[plan.where + b] = offset + r
            return c

        lax.fori_loop(1, count, one, 0)
        return p + count

    lax.fori_loop(0, g, group, jnp.int32(0))
    s = plan.scalars
    before, after, own = held[width + prev], held[width + nxt], held[width + me]
    tab[s + 0] = plan.order + held[start + prev]
    tab[s + 1] = before
    tab[s + 2] = total - before - own
    tab[s + 3] = plan.order + held[start + nxt] + after - 1 + total
    tab[s + 4] = after
    tab[s + 5] = total - after - 1
    tab[s + 6] = jnp.where(counts_ref[col] > me, 1, 0)


def step_kernel(
    plan,
    grads, left, right, momentum, tab,
    pieces, new_momentum,
    gp, gm, landp, landm, outp, outm, zp, zm, abuf, gblk,
    lv, rv, mv, inner, outer, nm, ubuf, cbuf, fbuf,
    sq_own, sq_mid, sqz, sqs, sq_sum,
    load_sem, ring_send, ring_recv, z_send, zp_recv, zm_recv, a_send, a_recv,
    q_send, q_recv, u_send, u_recv, f_send, f_recv,
    direct, zland, h_send, h_recv, g_send, g_recv,
    *rbufs,
):
    n, g, nb = plan.planes, plan.groups, plan.blocks
    rows, cols = plan.rows, plan.cols
    slab = rows // g
    half = slab // 2
    width = cols // n
    me, col = lax.axis_index("dp"), lax.axis_index("shard")
    ahead, behind = lax.rem(me + 1, n), lax.rem(me + n - 1, n)

    def loop(low, high, body):
        lax.fori_loop(low, high, lambda i, c: (body(i), c)[1], 0)

    def remote(src, dst, send, recv, dp, shard):
        return pltpu.make_async_remote_copy(
            src_ref=src, dst_ref=dst, send_sem=send, recv_sem=recv,
            device_id={"dp": dp, "shard": shard}, device_id_type=MESH,
        )

    load_p = pltpu.make_async_copy(grads.at[0, :, 0:half, :], gp.at[0:nb], load_sem.at[0])
    load_m = pltpu.make_async_copy(grads.at[0, :, half:slab, :], gm.at[0:nb], load_sem.at[1])
    load_p.start()
    load_m.start()
    loads = [
        pltpu.make_async_copy(src.at[0], dst, load_sem.at[2 + i])
        for i, (src, dst) in enumerate(((left, lv), (right, rv), (momentum, mv)))
    ]

    barrier = pltpu.get_barrier_semaphore()
    for a in range(1, n):
        pl.semaphore_signal(
            barrier, inc=1, device_id={"dp": lax.rem(me + a, n), "shard": col}, device_id_type=MESH
        )

    def greet(a):
        pl.semaphore_signal(
            barrier, inc=1, device_id={"dp": me, "shard": lax.rem(col + a, g)}, device_id_type=MESH
        )

    loop(1, g, greet)
    pl.semaphore_wait(barrier, n - 1 + g - 1)
    load_p.wait()
    load_m.wait()
    for load in loads:
        load.start()

    sc = plan.scalars
    ways = (
        (gp, landp, outp, 0, ahead, tab[sc], 1, tab[sc + 1]),
        (gm, landm, outm, 1, behind, tab[sc + 3], -1, tab[sc + 4]),
    )
    parts = tuple(slice(h * (cols // PARTS), (h + 1) * (cols // PARTS)) for h in range(PARTS))

    def passing(way, k, h):
        _, land, out, d, to, _, _, _ = way
        return remote(
            out.at[k, :, parts[h]], land.at[k, :, parts[h]],
            ring_send.at[d], ring_recv.at[PARTS * d + h, k], to, col,
        )

    def take(k, h):
        for way in ways:
            held, land, _, _, _, start, sign, lag = way
            passing(way, k, h).wait_recv()
            own = held[tab[jnp.maximum(start + sign * (lag + k), 0)], :, parts[h]]
            held[nb + k, :, parts[h]] = land[k, :, parts[h]] + own

    def give(k, h):
        for way in ways:
            held, _, out, _, _, start, sign, lag = way
            source = jnp.where(k < lag, tab[jnp.maximum(start + sign * k, 0)], nb + k - lag)
            out[k, :, parts[h]] = held[source, :, parts[h]]
            passing(way, k, h).start()

    def ring(k, taking=True, giving=True):
        for h in range(PARTS):
            if taking:
                take(k - LAG, h)
            if giving:
                give(k, h)

    def exchange(t):
        @pl.when(t == 0)
        def _():
            gblk[pl.ds(col * slab, slab), :] = abuf[0]

        @pl.when(t > 0)
        def _():
            remote(
                abuf.at[t], gblk.at[pl.ds(col * slab, slab), :], a_send, a_recv,
                me, lax.rem(t + col, g),
            ).start()

    def count_squares(t, counted):
        x = abuf[t].astype(F32)
        sq_sum[...] += jnp.where(counted, jnp.sum(x * x, axis=0, keepdims=True), 0.0)

    far = SKEW * (n - 1)
    lines = (
        (gp, zp, 0, zp_recv, ahead, me - 1, 1),
        (gm, zm, 1, zm_recv, behind, n - 1 - me, n - 1),
    )
    begin, ready = max(plan.sends - EARLY, LAG), plan.sends + LAG
    end = max(begin + far + g - LAG, ready + g)

    def along(line, q):
        _, zbuf, d, recv, to, _, _ = line
        return remote(zbuf.at[q], zbuf.at[q], z_send.at[d], recv.at[q], to, col)

    def first_block(line, q):
        return line[0][tab[plan.first + lax.rem(q + col, g)]]

    def chain(t):
        @pl.when(me != 0)
        def _():
            for line in lines:
                zbuf, hops, source = line[1], line[5], line[6]
                q = t - begin - SKEW * hops + LAG

                @pl.when((q >= LAG) & (q < g))
                def _():
                    @pl.when(me == source)
                    def _():
                        zbuf[q] = first_block(line, q)

                    @pl.when(me != source)
                    def _():
                        along(line, q).wait_recv()
                        zbuf[q] = zbuf[q] + first_block(line, q)

                    along(line, q).start()

        @pl.when((me == 0) & (t >= begin + far) & (t < begin + far + g - LAG))
        def _():
            q = t - begin - far + LAG
            for line, low in zip(lines, (0, half)):
                along(line, q).wait_recv()
                abuf[q, low:low + half, :] = line[1][q] + first_block(line, q)
            exchange(q)
            count_squares(q, True)

    def settle(t):
        i = t - ready

        @pl.when((i < g) & ((me != 0) | (i < LAG)))
        def _():
            listed = tab[plan.rank + lax.rem(i + col, g)]
            r = jnp.where(me == 0, i, jnp.maximum(listed, 0))
            abuf[i, 0:half, :] = gp[nb + tab[sc + 2] + r]
            abuf[i, half:slab, :] = gm[nb + tab[sc + 5] - r]
            exchange(i)
            count_squares(i, listed >= 0)

    sq_sum[...] = jnp.zeros_like(sq_sum)
    loop(0, LAG, lambda k: ring(k, taking=False))
    loop(LAG, begin, ring)
    loop(begin, plan.sends, lambda k: (ring(k), chain(k)))
    loop(plan.sends, ready, lambda k: (ring(k, giving=False), chain(k)))
    loop(ready, end, lambda k: (chain(k), settle(k)))

    sq_own[...] = jnp.full((8, 128), jnp.sum(sq_sum[...]), F32)
    sqz[me] = sq_own[...]
    for a in range(1, n):
        to = lax.rem(me + a, n)
        remote(sq_own, sqz.at[me], q_send.at[0], q_recv.at[0], to, col).start()

    remote(
        gblk.at[0:(g - 1) * slab], gblk.at[0:(g - 1) * slab], a_send, a_recv, me, col
    ).wait_recv()
    filled = tab[sc + 6] > 0
    tile = min(128, rows)
    for load in loads:
        load.wait()
    strip = 256

    def first_product(i, acc):
        at = pl.ds(pl.multiple_of(i * strip, strip), strip)
        inner[:, at] = jnp.dot(lv[...], gblk[:, at], preferred_element_type=F32).astype(BF16)
        x = gblk[:, at].astype(F32)
        return acc + jnp.sum(x * x, axis=0, keepdims=True)

    grad_square = jnp.sum(
        lax.fori_loop(0, cols // strip, first_product, jnp.zeros((1, strip), F32))
    )
    own_tile = jnp.full((8, 128), grad_square, F32)
    remote(sqz.at[0:n - 1], sqz.at[0:n - 1], q_send.at[0], q_recv.at[0], me, col).wait_recv()
    mid = sqz[0]
    for j in range(1, n):
        mid = mid + sqz[j]
    sq_mid[...] = mid
    sqs[col] = mid

    def tell(a):
        remote(
            sq_mid, sqs.at[col], q_send.at[1], q_recv.at[1], me, lax.rem(col + a, g)
        ).start()

    loop(1, g, tell)

    def second_product(i, acc):
        at = pl.ds(pl.multiple_of(i * strip, strip), strip)
        x = jnp.dot(inner[...], rv[:, at], preferred_element_type=F32)
        outer[:, at] = x
        return acc + jnp.sum(x * x, axis=0, keepdims=True)

    outer_square = jnp.sum(
        lax.fori_loop(0, cols // strip, second_product, jnp.zeros((1, strip), F32))
    )
    remote(sqs.at[0:g - 1], sqs.at[0:g - 1], q_send.at[1], q_recv.at[1], me, col).wait_recv()
    total = lax.fori_loop(0, g, lambda j, acc: acc + sqs[j], jnp.zeros((8, 128), F32))
    cells = float(rows * cols)
    outer_tile = jnp.full((8, 128), outer_square, F32)
    graft = (jnp.sqrt(own_tile / cells) * lax.rsqrt(outer_tile / cells + 1e-06))[0:1, :]
    clip = jnp.minimum(1.0, 0.5 * lax.rsqrt(total / (nb * cells) + 1e-06))[0:1, :]

    pairs = chunks_of(n)
    def home(a, j, to):
        return remote(
            cbuf.at[a, 0:plan.most[j]], fbuf.at[plan.base[j]:plan.base[j] + plan.most[j]],
            f_send.at[a], f_recv.at[j], to, col,
        )

    def step_of(at, a):
        lanes = pl.ds(pl.multiple_of(lax.rem(me + a, n) * width, width), width)
        direction = jnp.where(filled, clip * (graft * outer[at, lanes]), 0.0)
        following = 0.9 * mv[at, lanes].astype(F32) + direction
        nm[at, lanes] = following.astype(BF16)
        return (-0.8 * (0.9 * following + direction)).astype(BF16)

    def outward(q, pair):
        def part(i):
            at = pl.ds(pl.multiple_of(i * tile, tile), tile)
            for h, a in enumerate(pair):
                ubuf[q, at, h * width:(h + 1) * width] = step_of(at, a)

        loop(0, rows // tile, part)
        rbufs[q][col] = ubuf[q, pl.ds(col * slab, slab), 0:len(pair) * width]

        def back(a):
            to = lax.rem(col + a, g)
            remote(
                ubuf.at[q, pl.ds(to * slab, slab), 0:len(pair) * width], rbufs[q].at[col],
                u_send.at[q], u_recv.at[q], me, to,
            ).start()

        loop(1, g, back)

    def homeward(q, pair):
        remote(
            rbufs[q].at[0:g - 1], rbufs[q].at[0:g - 1], u_send.at[q], u_recv.at[q], me, col
        ).wait_recv()

        def gather(r):
            piece = rbufs[q][tab[plan.slot + r]]
            for h, a in enumerate(pair):
                cbuf[a, r] = piece[:, h * width:(h + 1) * width]

        loop(0, g, gather)
        for j in range(1, n):
            @pl.when(me == j)
            def _():
                for a in pair:
                    if a == 0:
                        fbuf[plan.base[j]:plan.base[j] + plan.most[j]] = (
                            cbuf[a, 0:plan.most[j]]
                        )
                    else:
                        home(a, j, lax.rem(me + a, n)).start()

    store = pltpu.make_async_copy(nm, new_momentum.at[0], load_sem.at[5])

    def across(a):
        return remote(direct.at[a], zland, h_send.at[a], h_recv, lax.rem(me + a, n), col)

    def scatter():
        fbuf[col] = zland[pl.ds(col * slab, slab), :]

        def drop(a):
            to = lax.rem(col + a, g)
            remote(
                zland.at[pl.ds(to * slab, slab), :], fbuf.at[col], g_send, g_recv, me, to
            ).start()

        loop(1, g, drop)

    @pl.when(me == 0)
    def _():
        for a in plane_order(n):
            def part(i):
                at = pl.ds(pl.multiple_of(i * tile, tile), tile)
                if a == 0:
                    zland[at, :] = step_of(at, a)
                else:
                    direct[a, at, :] = step_of(at, a)

            loop(0, rows // tile, part)
            if a != 0:
                across(a).start()
        store.start()
        scatter()

    @pl.when(me != 0)
    def _():
        for q, pair in enumerate(pairs):
            outward(q, pair)
            if q > 0:
                homeward(q - 1, pairs[q - 1])
        store.start()
        across(0).wait_recv()
        scatter()
        homeward(len(pairs) - 1, pairs[-1])

    for j in range(1, n):
        @pl.when(me != j)
        def _():
            home(0, j, me).wait_recv()

    scattered = remote(fbuf.at[0:g - 1], fbuf.at[0:g - 1], g_send, g_recv, me, col)
    scattered.wait_recv()

    keep = pltpu.make_async_copy(fbuf, pieces, load_sem.at[0])
    keep.start()
    store.wait()
    keep.wait()
    for way in ways:
        remote(way[2], way[1], ring_send.at[way[3]], ring_recv.at[0, 0], me, col).wait_send()

    @pl.when(me != 0)
    def _():
        for line in lines:
            remote(
                line[1].at[LAG:g], line[1].at[LAG:g], z_send.at[line[2]], line[3].at[0], me, col
            ).wait_send()

    remote(abuf.at[1:g], abuf.at[1:g], a_send, a_recv, me, col).wait_send()
    remote(sqz.at[0:n - 1], sqz.at[0:n - 1], q_send.at[0], q_recv.at[0], me, col).wait_send()
    remote(sqs.at[0:g - 1], sqs.at[0:g - 1], q_send.at[1], q_recv.at[1], me, col).wait_send()
    scattered.wait_send()

    @pl.when(me == 0)
    def _():
        for a in range(1, n):
            across(a).wait_send()

    @pl.when(me != 0)
    def _():
        for q in range(len(pairs)):
            remote(
                rbufs[q].at[0:g - 1], rbufs[q].at[0:g - 1], u_send.at[q], u_recv.at[q], me, col
            ).wait_send()

    for j in range(1, n):
        @pl.when(me == j)
        def _():
            for a in range(1, n):
                home(a, j, me).wait_send()


def last_kernel(plan, pieces, following, tab, update, new_momentum, through, held, placed, sems):
    step = plan.rows // 4
    rows = [slice(i * step, (i + 1) * step) for i in range(4)]
    fetch = pltpu.make_async_copy(pieces, held, sems.at[8])
    reads = [
        pltpu.make_async_copy(following.at[0, r], through.at[r], sems.at[i])
        for i, r in enumerate(rows)
    ]
    writes = [
        pltpu.make_async_copy(through.at[r], new_momentum.at[0, r], sems.at[4 + i])
        for i, r in enumerate(rows)
    ]
    fetch.start()
    for read in reads:
        read.start()
    fetch.wait()

    def place(b, c):
        placed[b] = held[tab[plan.where + b]]
        return c

    lax.fori_loop(0, plan.blocks, place, 0)
    put = pltpu.make_async_copy(placed, update, sems.at[9])
    put.start()
    for read, write in zip(reads, writes):
        read.wait()
        write.start()
    for write in writes:
        write.wait()
    put.wait()


def per_device(planes, groups, grads, left, right, momentum, block_order, owner_counts):
    blocks, slab, cols = grads.shape[1:]
    rows = left.shape[1]
    plan = Plan(planes, groups, blocks, rows, cols)
    half, width = slab // 2, cols // planes
    smem = pl.BlockSpec(memory_space=pltpu.SMEM)
    table = pl.pallas_call(
        functools.partial(table_kernel, plan),
        out_shape=jax.ShapeDtypeStruct((plan.size,), jnp.int32),
        in_specs=[smem, smem],
        out_specs=smem,
        scratch_shapes=[pltpu.SMEM((64,), jnp.int32)],
    )(block_order, owner_counts)
    anywhere = pl.BlockSpec(memory_space=pl.ANY)
    dma = pltpu.SemaphoreType.DMA
    held = plan.blocks + plan.sends
    chunks = chunks_of(planes)
    pieces, following = pl.pallas_call(
        functools.partial(step_kernel, plan),
        out_shape=(
            jax.ShapeDtypeStruct((plan.slots, slab, width), BF16),
            jax.ShapeDtypeStruct((1, rows, cols), BF16),
        ),
        in_specs=[anywhere] * 4 + [smem],
        out_specs=(anywhere, anywhere),
        scratch_shapes=(
            [pltpu.VMEM((held, half, cols), BF16)] * 2
            + [pltpu.VMEM((plan.sends, half, cols), BF16)] * 4
            + [pltpu.VMEM((groups, half, cols), BF16)] * 2
            + [pltpu.VMEM((groups, slab, cols), BF16), pltpu.VMEM((rows, cols), BF16)]
            + [
                pltpu.VMEM((rows, rows), BF16),
                pltpu.VMEM((cols, cols), BF16),
                pltpu.VMEM((rows, cols), BF16),
                pltpu.VMEM((rows, cols), BF16),
                pltpu.VMEM((rows, cols), F32),
                pltpu.VMEM((rows, cols), BF16),
                pltpu.VMEM((len(chunks), rows, 2 * width), BF16),
                pltpu.VMEM((planes, groups, slab, width), BF16),
                pltpu.VMEM((plan.slots, slab, width), BF16),
                pltpu.VMEM((8, 128), F32),
                pltpu.VMEM((8, 128), F32),
                pltpu.VMEM((planes, 8, 128), F32),
                pltpu.VMEM((groups, 8, 128), F32),
                pltpu.VMEM((1, cols), F32),
            ]
            + [
                dma((6,)),
                dma((2,)),
                dma((2 * PARTS, plan.sends)),
                dma((2,)),
                dma((groups,)),
                dma((groups,)),
                dma,
                dma,
                dma((2,)),
                dma((2,)),
                dma((len(chunks),)),
                dma((len(chunks),)),
                dma((planes,)),
                dma((planes,)),
                pltpu.VMEM((planes, rows, width), BF16),
                pltpu.VMEM((rows, width), BF16),
                dma((planes,)),
                dma,
                dma,
                dma,
            ]
            + [pltpu.VMEM((groups, slab, len(c) * width), BF16) for c in chunks]
        ),
        compiler_params=pltpu.CompilerParams(
            collective_id=0, has_side_effects=True, vmem_limit_bytes=56 * 1024 * 1024
        ),
        cost_estimate=pl.CostEstimate(
            flops=2 * rows * cols * (rows + cols), bytes_accessed=2 * 13 * rows * cols // 2,
            transcendentals=0,
        ),
    )(grads, left, right, momentum, table)
    return pl.pallas_call(
        functools.partial(last_kernel, plan),
        out_shape=(
            jax.ShapeDtypeStruct((blocks, slab, width), BF16),
            jax.ShapeDtypeStruct((1, rows, cols), BF16),
        ),
        in_specs=[anywhere, anywhere, smem],
        out_specs=(anywhere, anywhere),
        scratch_shapes=[
            pltpu.VMEM((rows, cols), BF16),
            pltpu.VMEM((plan.slots, slab, width), BF16),
            pltpu.VMEM((blocks, slab, width), BF16),
            dma((10,)),
        ],
    )(pieces, following, table)


def solution(mesh):
    slots = P(("dp", "shard"), None, None)
    return jax.shard_map(
        functools.partial(per_device, mesh.shape["dp"], mesh.shape["shard"]),
        mesh=mesh,
        in_specs=(P("dp", None, "shard", None), slots, slots, slots, P(), P()),
        out_specs=(P(None, "shard", "dp"), slots),
        check_vma=False,
    )
```
